1024 devices in a mesh: blk: 64 (over y, z), lev: 16 (over x, core).
Axes of the slice: x: 8, y: 8, z: 8, core: 2. Of those that a mesh axis runs over, the one named last changes fastest.
Arguments:
- io_data: bfloat16 [7, 128, 32768], P(None, 'lev', 'blk'), may hold values from -6 to 6
- io_map: int32 [32768], P('blk'), may hold values from 0 to 32767, as said below
- phys_map: int32 [32768], P('blk'), may hold values from 0 to 32767, as said below
- neighbours: int32 [4, 32768], P(None, 'blk'), may hold values from 0 to 32767, as said below
- column_op: bfloat16 [896, 896], replicated, may hold values from -0.1875 to 0.1875
Outputs:
- tendency: float32 [32768, 7, 128], P(('blk', 'lev'))
The draws below stay inside these ranges and needn't reach their ends.
Inputs may be any that keep to these rules, and one draw needn't show every extreme that they name: `io_map`: A permutation. The number of positions of block s (positions s * 512 to (s + 1) * 512 - 1) whose image lies in block d depends only on (d - s) modulo the number of blocks, is at most 16, and is exactly 16 for d = s. `phys_map`: A permutation with the same properties as io_map, from element blocks to physics blocks. `neighbours`: each entry is its column's index plus an offset of 1 to 32 in magnitude, modulo 32768; offsets 32 and -32 occur in every block.
All inputs are finite; a program needn't handle non-finite values.
Results may differ from the reference program's by a relative error of at most 0.0029.
Values may be sent and summed in bfloat16 or wider, within the bound.
A program may use at most 32 MiB of HBM per device.

```python
import jax
import jax.numpy as jnp

FIELDS = 7
C_DEV = 512
HALO = 32
CAP = 16
LEVELS = 128
COLUMNS = 32768
N_BLK = 64


def spread_map(key):
    key_pair, key_order, key_src, key_dst = jax.random.split(key, 4)
    pairs = jax.random.randint(key_pair, (N_BLK // 2,), 0, CAP + 1).astype(jnp.int32)
    weights = jnp.stack([pairs, CAP - pairs], axis=1).reshape(-1)
    weights = weights.at[0].set(CAP).at[1].set(0)
    order = jnp.concatenate([jnp.zeros((1,), jnp.int32), 1 + jax.random.permutation(key_order, N_BLK - 1).astype(jnp.int32)])
    counts = jnp.zeros((N_BLK,), jnp.int32).at[order].set(weights)
    ends = jnp.cumsum(counts).astype(jnp.int32)
    source_perm = jax.vmap(lambda k: jax.random.permutation(k, C_DEV))(jax.random.split(key_src, N_BLK)).astype(jnp.int32)
    dest_perm = jax.vmap(lambda k: jax.random.permutation(k, C_DEV))(jax.random.split(key_dst, N_BLK)).astype(jnp.int32)
    segment = jnp.sum((ends[None, None, :] <= source_perm[:, :, None]).astype(jnp.int32), axis=2)
    source = jnp.arange(N_BLK, dtype=jnp.int32)[:, None]
    dest = (source + segment) % N_BLK
    value = dest * C_DEV + dest_perm[dest, source_perm]
    return value.reshape(-1).astype(jnp.int32)


def draw_io_map(key, part):
    key = jax.random.fold_in(key, 11)
    return spread_map(key)


def draw_phys_map(key, part):
    key = jax.random.fold_in(key, 23)
    return spread_map(key)


def draw_neighbours(key, part):
    key = jax.random.fold_in(key, 37)
    key_mag, key_sign = jax.random.split(key)
    column = jnp.arange(COLUMNS, dtype=jnp.int32)[None, :]
    magnitude = jax.random.randint(key_mag, (4, COLUMNS), 1, HALO + 1)
    sign = jax.random.randint(key_sign, (4, COLUMNS), 0, 2) * 2 - 1
    offset = (magnitude * sign).astype(jnp.int32)
    which = jnp.arange(4, dtype=jnp.int32)[:, None]
    offset = jnp.where((which == 0) & (column % C_DEV == 0), -HALO, offset)
    offset = jnp.where((which == 1) & (column % C_DEV == C_DEV - 1), HALO, offset)
    return ((column + offset) % COLUMNS).astype(jnp.int32)


def level_of(key, shape, shards, smallest, high):
    gain, own = 1.0, jax.random.fold_in(key, 6)
    for axis_at, parts in shards:
        steps = jnp.exp(jax.random.uniform(jax.random.fold_in(own, axis_at), (parts,), jnp.float32, smallest / len(shards), high / len(shards)))
        gain = gain * jnp.repeat(steps, shape[axis_at] // parts).reshape([-1 if axis == axis_at else 1 for axis in range(len(shape))])
    return gain


def normal_values(key, dims, scale, most, cuts=(), held_as=jnp.bfloat16):
    entries = jax.random.normal(key, dims, jnp.float32) * scale
    if len(cuts) > 0:
        entries = level_of(key, dims, cuts, -0.22, 0.18) * entries
    return jnp.clip(entries, min=-most, max=most).astype(held_as)


def setup_inputs(seed: int = 0) -> dict:
    keys = jax.random.split(jax.random.key(seed), 6)
    io_data = normal_values(keys[0], (FIELDS, LEVELS, COLUMNS), 1.0, 6.0, ((1, 16), (2, 64)))
    io_map = draw_io_map(jax.random.fold_in(keys[5], 71), 0)
    phys_map = draw_phys_map(jax.random.fold_in(keys[5], 71), 0)
    neighbours = draw_neighbours(jax.random.fold_in(keys[5], 71), 0)
    column_op = normal_values(keys[4], (FIELDS * LEVELS, FIELDS * LEVELS), (FIELDS * LEVELS) ** -0.5, 0.1875)
    return {"io_data": io_data, "io_map": io_map, "phys_map": phys_map, "neighbours": neighbours, "column_op": column_op}


def reference(io_data, io_map, phys_map, neighbours, column_op):
    dynamics = jnp.zeros_like(io_data).at[:, :, io_map].set(io_data)
    values = dynamics.astype(jnp.float32)
    beside_all = values[:, :, neighbours[0]]
    for index in range(1, 4):
        beside_all = beside_all + values[:, :, neighbours[index]]
    stepped = (values + 0.2 * (beside_all - 4.0 * values)).astype(jnp.bfloat16)
    physics = jnp.zeros_like(stepped).at[:, :, phys_map].set(stepped)
    columns = physics.reshape(FIELDS * LEVELS, COLUMNS)
    result = jnp.dot(columns.T, column_op, preferred_element_type=jnp.float32)
    return result.reshape(COLUMNS, FIELDS, LEVELS)
```

```python
import functools

import jax
import jax.numpy as jnp
from jax import lax
from jax.experimental import pallas as pl
from jax.experimental.pallas import tpu as pltpu
from jax.sharding import PartitionSpec as P

HALO = 32
CAP = 16
HALF = CAP // 2
LANES = 128
SIDE = LANES // 2
MESH = pl.DeviceIdType.MESH
F32 = jnp.float32
BF16 = jnp.bfloat16
I32 = jnp.int32


def dot_nn(left, right):
    return lax.dot_general(left, right, (((1,), (0,)), ((), ())), preferred_element_type=F32)


def dot_nt(left, right):
    return lax.dot_general(left, right, (((1,), (1,)), ((), ())), preferred_element_type=F32)


def onehot(mask):
    return jnp.where(mask, 1.0, 0.0).astype(BF16)


def rows_of(shape):
    return lax.broadcasted_iota(I32, shape, 0)


def lanes_of(shape):
    return lax.broadcasted_iota(I32, shape, 1)


def both_sides(stack):
    turned = pltpu.roll(stack, SIDE, 1)
    first = lanes_of(stack.shape) < SIDE
    return jnp.where(first, stack, turned).astype(BF16), jnp.where(first, turned, stack).astype(BF16)


def kernel(
    blocks, levs,
    io_hbm, io_map_hbm, phys_map_hbm, near_hbm, op_hbm,
    out_ref,
    io_v, io_map_v, phys_map_v, near_v, op_v, weight,
    pick_lo, pick_hi, step_lo, step_hi, place_lo, place_hi, cells, halo,
    out_a, in_a, out_c, in_c, out_d, in_d, columns,
    load_sem, op_sem, sems, halo_sems,
):
    fields, lev_dev, width = io_v.shape
    rows = blocks * HALF
    total = blocks * width
    shift = width.bit_length() - 1
    me = lax.axis_index("blk")
    my_lev = lax.axis_index("lev")

    loads = [
        pltpu.make_async_copy(src, dst, load_sem.at[at])
        for at, (src, dst) in enumerate(
            ((io_map_hbm, io_map_v), (phys_map_hbm, phys_map_v), (io_hbm, io_v), (near_hbm, near_v))
        )
    ]
    for load in loads:
        load.start()

    barrier = pltpu.get_barrier_semaphore()

    def greet_blk(k, carry):
        pl.semaphore_signal(
            barrier, inc=1, device_id=((me + k) & (blocks - 1), my_lev), device_id_type=MESH
        )
        return carry

    def greet_lev(k, carry):
        pl.semaphore_signal(
            barrier, inc=1, device_id=(me, (my_lev + k) & (levs - 1)), device_id_type=MESH
        )
        return carry

    lax.fori_loop(1, blocks, greet_blk, 0)
    lax.fori_loop(1, levs, greet_lev, 0)

    def load_op(l, carry):
        pltpu.make_async_copy(op_hbm.at[:, l], op_v.at[l, pl.ds(0, fields)], op_sem).start()
        return carry

    lax.fori_loop(0, levs, load_op, 0)

    loads[0].wait()
    loads[1].wait()
    codes = []
    members = []
    for ref in (io_map_v, phys_map_v):
        offset = ((ref[...] >> shift) - me) & (blocks - 1)
        members.append((offset, rows_of((blocks, width)) == offset))
    before = onehot(rows_of((width, width)) < lanes_of((width, width)))
    ranked = dot_nn(
        jnp.concatenate([onehot(members[0][1]), onehot(members[1][1])], axis=0), before
    )
    for at, (offset, member) in enumerate(members):
        part = ranked[at * blocks : (at + 1) * blocks]
        rank = jnp.sum(jnp.where(member, part, 0.0), axis=0, keepdims=True).astype(I32)
        code = offset * HALF + rank
        codes.append(
            (jnp.where(rank < HALF, code, -1), jnp.where(rank >= HALF, code - HALF, -1))
        )

    loads[2].wait()
    meta_row = rows_of((8, width))

    def meta(ref, first):
        slot = (ref[...] & (width - 1)) + 1
        high = (slot >> 5).astype(F32)
        low = (slot & 31).astype(F32)
        return jnp.where(meta_row == first, high, jnp.where(meta_row == first + 1, low, 0.0))

    data = io_v[...].astype(F32).reshape(fields * lev_dev, width)
    one = jnp.concatenate([data, meta(io_map_v, 0)], axis=0)
    own = jnp.concatenate([one, one], axis=0).astype(BF16)
    one = jnp.concatenate([jnp.zeros_like(data), meta(phys_map_v, 2)], axis=0)
    later = jnp.concatenate([one, one], axis=0).astype(BF16)

    where_row = rows_of((rows, width))
    pick_lo[...] = onehot(where_row == codes[1][0])
    pick_hi[...] = onehot(where_row == codes[1][1])
    first_side = lanes_of((rows, LANES)) < SIDE
    lo = dot_nt(onehot(where_row == codes[0][0]), own) + dot_nt(pick_lo[...], later)
    hi = dot_nt(onehot(where_row == codes[0][1]), own) + dot_nt(pick_hi[...], later)
    out_a[...] = jnp.where(first_side, lo, hi).reshape(blocks, HALF, LANES).astype(BF16)

    pl.semaphore_wait(barrier, blocks - 1 + levs - 1)

    def blk_send(src, dst, at):
        def send(k, carry):
            pltpu.make_async_remote_copy(
                src_ref=src.at[k],
                dst_ref=dst.at[k],
                send_sem=sems.at[at],
                recv_sem=sems.at[at + 1],
                device_id=((me + k) & (blocks - 1), my_lev),
                device_id_type=MESH,
            ).start()
            return carry

        lax.fori_loop(1, blocks, send, 0)
        dst[0] = src[0]

    def blk_wait(src, dst, at):
        return pltpu.make_async_remote_copy(
            src_ref=src.at[pl.ds(1, blocks - 1)],
            dst_ref=dst.at[pl.ds(1, blocks - 1)],
            send_sem=sems.at[at],
            recv_sem=sems.at[at + 1],
            device_id=((me + 1) & (blocks - 1), my_lev),
            device_id_type=MESH,
        )

    blk_send(out_a, in_a, 0)

    loads[3].wait()
    near = (near_v[...] - me * width + HALO) & (total - 1)
    near = jnp.where(
        near < HALO, near + width, jnp.where(near < width + HALO, near - HALO, near)
    )
    wide = (width + 2 * HALO, width)
    spot = rows_of(wide)
    taps = jnp.where(spot == lanes_of(wide), 1.0, 0.0)
    for index in range(4):
        taps = taps + jnp.where(spot == near[index : index + 1], 1.0, 0.0)
    taps = taps.astype(BF16)
    step_lo[...] = dot_nt(pick_lo[...], taps).astype(BF16)
    step_hi[...] = dot_nt(pick_hi[...], taps).astype(BF16)

    pltpu.make_async_copy(
        op_v.at[:, pl.ds(0, fields)], op_v.at[:, pl.ds(0, fields)], op_sem
    ).wait()
    depth = SIDE

    def spread(l, carry):
        block = op_v[l].astype(F32)
        block = jnp.where(
            lax.broadcasted_iota(I32, block.shape, 0) < fields, block, 0.0
        ).reshape(depth, block.shape[2])
        weight[pl.ds(pl.multiple_of(l * depth, depth), depth), :] = block.astype(BF16)
        return carry

    lax.fori_loop(0, levs, spread, 0)

    blk_wait(out_a, in_a, 0).wait_recv()
    stack = in_a[...].astype(F32).reshape(rows, LANES)
    choose_row = rows_of((8, LANES))
    choose_lane = lanes_of((8, LANES))
    choose = jnp.zeros((8, LANES), F32)
    for at, lane in enumerate((56, 56 + SIDE, 58, 58 + SIDE)):
        here = choose_row == at
        choose = jnp.where(here & (choose_lane == lane), 32.0, choose)
        choose = jnp.where(here & (choose_lane == lane + 1), 1.0, choose)
    slots = dot_nt(choose.astype(BF16), stack.astype(BF16)).astype(I32)
    left, right = both_sides(stack)
    target = rows_of((width, rows)) + 1
    found = dot_nn(onehot(target == slots[0:1]), left) + dot_nn(onehot(target == slots[1:2]), right)
    cells[...] = found.astype(BF16)

    down = pltpu.make_async_remote_copy(
        src_ref=cells.at[pl.ds(0, HALO)],
        dst_ref=halo.at[pl.ds(HALO, HALO)],
        send_sem=halo_sems.at[0],
        recv_sem=halo_sems.at[1],
        device_id=((me + blocks - 1) & (blocks - 1), my_lev),
        device_id_type=MESH,
    )
    up = pltpu.make_async_remote_copy(
        src_ref=cells.at[pl.ds(width - HALO, HALO)],
        dst_ref=halo.at[pl.ds(0, HALO)],
        send_sem=halo_sems.at[2],
        recv_sem=halo_sems.at[3],
        device_id=((me + 1) & (blocks - 1), my_lev),
        device_id_type=MESH,
    )
    down.start()
    up.start()

    lo = dot_nn(step_lo[:, :width], cells[...])
    hi = dot_nn(step_hi[:, :width], cells[...])
    per = levs * CAP
    line = rows_of((per, rows))
    line = (line >> 4) * (2 * CAP) + (line & (CAP - 1)) + 1
    place_lo[pl.ds(0, per), :] = onehot(line == slots[2:3])
    place_hi[pl.ds(0, per), :] = onehot(line == slots[3:4])
    place_lo[pl.ds(per, per), :] = onehot(line + CAP == slots[2:3])
    place_hi[pl.ds(per, per), :] = onehot(line + CAP == slots[3:4])

    down.wait_recv()
    up.wait_recv()
    lo = lo + dot_nn(step_lo[:, width:], halo[...])
    hi = hi + dot_nn(step_hi[:, width:], halo[...])
    out_c[...] = (0.2 * jnp.where(first_side, lo, hi)).reshape(blocks, HALF, LANES).astype(BF16)
    blk_send(out_c, in_c, 2)

    blk_wait(out_c, in_c, 2).wait_recv()
    left, right = both_sides(in_c[...].astype(F32).reshape(rows, LANES))
    placed = dot_nn(place_lo[...], left) + dot_nn(place_hi[...], right)
    out_d[...] = (
        jnp.where(lanes_of((per, LANES)) < SIDE, placed[:per], placed[per:])
        .reshape(levs, CAP, LANES).astype(BF16)
    )

    def lev_send(k, carry):
        to = (my_lev + k) & (levs - 1)
        pltpu.make_async_remote_copy(
            src_ref=out_d.at[to],
            dst_ref=in_d.at[my_lev],
            send_sem=sems.at[4],
            recv_sem=sems.at[5],
            device_id=(me, to),
            device_id_type=MESH,
        ).start()
        return carry

    lax.fori_loop(1, levs, lev_send, 0)
    in_d[my_lev] = out_d[my_lev]
    lev_wait = pltpu.make_async_remote_copy(
        src_ref=out_d.at[pl.ds(1, levs - 1)],
        dst_ref=in_d.at[pl.ds(1, levs - 1)],
        send_sem=sems.at[4],
        recv_sem=sems.at[5],
        device_id=(me, (my_lev + 1) & (levs - 1)),
        device_id_type=MESH,
    )
    lev_wait.wait_recv()
    side = lanes_of((CAP, LANES)) < SIDE
    for pair in range(levs // 2):
        even = in_d[2 * pair].astype(F32)
        odd = in_d[2 * pair + 1].astype(F32)
        upper = jnp.where(side, even, pltpu.roll(odd, SIDE, 1))
        lower = jnp.where(side, pltpu.roll(even, SIDE, 1), odd)
        columns[:, pair * LANES : (pair + 1) * LANES] = jnp.concatenate(
            [upper, lower], axis=0
        ).astype(BF16)
    result = dot_nn(columns[...], weight[...])
    size = levs * lev_dev
    for field in range(fields):
        out_ref[field] = result[:, field * size : (field + 1) * size]

    blk_wait(out_a, in_a, 0).wait_send()
    down.wait_send()
    up.wait_send()
    blk_wait(out_c, in_c, 2).wait_send()
    lev_wait.wait_send()


def local(io_data, io_map, phys_map, neighbours, column_op):
    fields, lev_dev, width = io_data.shape
    blocks = lax.axis_size("blk")
    levs = lax.axis_size("lev")
    rows = blocks * HALF
    count = width // levs
    span = fields * levs * lev_dev
    any_space = pl.BlockSpec(memory_space=pl.ANY)
    result = pl.pallas_call(
        functools.partial(kernel, blocks, levs),
        out_shape=jax.ShapeDtypeStruct((fields, count, levs * lev_dev), F32),
        in_specs=[any_space] * 5,
        out_specs=pl.BlockSpec(memory_space=pltpu.VMEM),
        scratch_shapes=[
            pltpu.VMEM((fields, lev_dev, width), BF16),
            pltpu.VMEM((1, width), I32),
            pltpu.VMEM((1, width), I32),
            pltpu.VMEM((4, width), I32),
            pltpu.VMEM((levs, fields + 1, lev_dev, span), BF16),
            pltpu.VMEM((levs * SIDE, span), BF16),
            pltpu.VMEM((rows, width), BF16),
            pltpu.VMEM((rows, width), BF16),
            pltpu.VMEM((rows, width + 2 * HALO), BF16),
            pltpu.VMEM((rows, width + 2 * HALO), BF16),
            pltpu.VMEM((width, rows), BF16),
            pltpu.VMEM((width, rows), BF16),
            pltpu.VMEM((width, LANES), BF16),
            pltpu.VMEM((2 * HALO, LANES), BF16),
            pltpu.VMEM((blocks, HALF, LANES), BF16),
            pltpu.VMEM((blocks, HALF, LANES), BF16),
            pltpu.VMEM((blocks, HALF, LANES), BF16),
            pltpu.VMEM((blocks, HALF, LANES), BF16),
            pltpu.VMEM((levs, CAP, LANES), BF16),
            pltpu.VMEM((levs, CAP, LANES), BF16),
            pltpu.VMEM((count, levs * SIDE), BF16),
            pltpu.SemaphoreType.DMA((4,)),
            pltpu.SemaphoreType.DMA,
            pltpu.SemaphoreType.DMA((6,)),
            pltpu.SemaphoreType.DMA((4,)),
        ],
        compiler_params=pltpu.CompilerParams(
            collective_id=0, has_side_effects=True, vmem_limit_bytes=48 * 1024 * 1024
        ),
    )(
        io_data,
        io_map.reshape(1, width),
        phys_map.reshape(1, width),
        neighbours,
        column_op.reshape(fields, levs, lev_dev, span),
    )
    return jnp.transpose(result, (1, 0, 2))


def solution(mesh):
    placed = (P(None, "lev", "blk"), P("blk"), P("blk"), P(None, "blk"), P())
    return jax.shard_map(
        local, mesh=mesh, in_specs=placed, out_specs=P(("blk", "lev"), None, None), check_vma=False
    )
```

```python
import functools

import jax
import jax.numpy as jnp
from jax import lax
from jax.experimental import pallas as pl
from jax.experimental.pallas import tpu as pltpu
from jax.sharding import PartitionSpec as P

HALO = 32
CAP = 16
HALF = CAP // 2
LANES = 128
SIDE = LANES // 2
MESH = pl.DeviceIdType.MESH
F32 = jnp.float32
BF16 = jnp.bfloat16
I32 = jnp.int32


def dot_nn(left, right):
    return lax.dot_general(left, right, (((1,), (0,)), ((), ())), preferred_element_type=F32)


def dot_nt(left, right):
    return lax.dot_general(left, right, (((1,), (1,)), ((), ())), preferred_element_type=F32)


def onehot(mask):
    return jnp.where(mask, 1.0, 0.0).astype(BF16)


def rows_of(shape):
    return lax.broadcasted_iota(I32, shape, 0)


def lanes_of(shape):
    return lax.broadcasted_iota(I32, shape, 1)


def both_sides(stack):
    turned = pltpu.roll(stack, SIDE, 1)
    first = lanes_of(stack.shape) < SIDE
    return jnp.where(first, stack, turned).astype(BF16), jnp.where(first, turned, stack).astype(BF16)


def ring(offset, count):
    return min(offset, count - offset)


def kernel(
    blocks, levs,
    io_hbm, io_map_hbm, phys_map_hbm, near_hbm, op_hbm,
    out_ref,
    io_v, io_map_v, phys_map_v, near_v, op_v, weight,
    pick_lo, pick_hi, step_lo, step_hi, step_halo, place_lo, place_hi, cells, halo, partial,
    out_a, in_a, out_c, in_c, out_d, in_d,
    load_sem, op_sem, sems, halo_sems, lev_sems,
):
    fields, lev_dev, width = io_v.shape
    rows = blocks * HALF
    total = blocks * width
    shift = width.bit_length() - 1
    me = lax.axis_index("blk")
    my_lev = lax.axis_index("lev")
    side_z = 1 << ((blocks.bit_length() - 1) // 2)
    side_y = blocks // side_z
    shift_z = side_z.bit_length() - 1
    my_y = me >> shift_z
    my_z = me & (side_z - 1)
    chips = levs // 2
    quarter = side_y // 4
    half_tiles = blocks // 2
    half = half_tiles * HALF
    offsets = sorted(
        ((y, z) for y in range(side_y) for z in range(side_z) if y or z),
        key=lambda at: (-ring(at[0], side_y) - ring(at[1], side_z), at),
    )
    lev_offsets = sorted(
        ((x, core) for x in range(chips) for core in range(2) if x or core),
        key=lambda at: (-ring(at[0], chips), at),
    )
    own_tile = quarter * side_z

    def tile_of(y, z):
        return ((y + quarter) % side_y) * side_z + z

    def at_blk(y, z):
        there = (((my_y + y) & (side_y - 1)) << shift_z) | ((my_z + z) & (side_z - 1))
        return there, my_lev

    def at_lev(x, core):
        return (((my_lev >> 1) + x) & (chips - 1)) * 2 + ((my_lev & 1) ^ core)

    barrier = pltpu.get_barrier_semaphore()
    for y, z in offsets:
        pl.semaphore_signal(barrier, inc=1, device_id=at_blk(y, z), device_id_type=MESH)
    for x, core in lev_offsets:
        pl.semaphore_signal(barrier, inc=1, device_id=(me, at_lev(x, core)), device_id_type=MESH)

    loads = [
        pltpu.make_async_copy(src, dst, load_sem.at[at])
        for at, (src, dst) in enumerate(
            ((io_map_hbm, io_map_v), (phys_map_hbm, phys_map_v), (io_hbm, io_v), (near_hbm, near_v))
        )
    ]
    for load in loads:
        load.start()

    def load_op(l, carry):
        pltpu.make_async_copy(op_hbm.at[:, l], op_v.at[l, pl.ds(0, fields)], op_sem).start()
        return carry

    lax.fori_loop(0, levs, load_op, 0)

    loads[0].wait()
    loads[1].wait()
    codes = []
    members = []
    for ref in (io_map_v, phys_map_v):
        owner = ref[...] >> shift
        to_y = ((owner >> shift_z) - my_y + quarter) & (side_y - 1)
        to_z = ((owner & (side_z - 1)) - my_z) & (side_z - 1)
        tile = (to_y << shift_z) | to_z
        members.append((tile, rows_of((blocks, width)) == tile))
    before = onehot(rows_of((width, width)) < lanes_of((width, width)))
    ranked = dot_nn(
        jnp.concatenate([onehot(members[0][1]), onehot(members[1][1])], axis=0), before
    )
    for at, (tile, member) in enumerate(members):
        part = ranked[at * blocks : (at + 1) * blocks]
        rank = jnp.sum(jnp.where(member, part, 0.0), axis=0, keepdims=True).astype(I32)
        code = tile * HALF + rank
        codes.append(
            (jnp.where(rank < HALF, code, -1), jnp.where(rank >= HALF, code - HALF, -1))
        )

    loads[2].wait()
    meta_row = rows_of((8, width))

    def meta(ref, first):
        slot = (ref[...] & (width - 1)) + 1
        high = (slot >> 5).astype(F32)
        low = (slot & 31).astype(F32)
        return jnp.where(meta_row == first, high, jnp.where(meta_row == first + 1, low, 0.0))

    data = io_v[...].astype(F32).reshape(fields * lev_dev, width)
    one = jnp.concatenate([data, meta(io_map_v, 0)], axis=0)
    own = jnp.concatenate([one, one], axis=0).astype(BF16)
    one = jnp.concatenate([jnp.zeros_like(data), meta(phys_map_v, 2)], axis=0)
    later = jnp.concatenate([one, one], axis=0).astype(BF16)

    where_row = rows_of((rows, width))
    pick_lo[...] = onehot(where_row == codes[1][0])
    pick_hi[...] = onehot(where_row == codes[1][1])
    first_side = lanes_of((rows, LANES)) < SIDE
    lo = dot_nt(onehot(where_row == codes[0][0]), own) + dot_nt(pick_lo[...], later)
    hi = dot_nt(onehot(where_row == codes[0][1]), own) + dot_nt(pick_hi[...], later)
    out_a[...] = jnp.where(first_side, lo, hi).reshape(blocks, HALF, LANES).astype(BF16)

    pl.semaphore_wait(barrier, blocks - 1 + levs - 1)

    def blk_copy(src, dst, at, far, first, count, to):
        return pltpu.make_async_remote_copy(
            src_ref=src.at[pl.ds(first, count)],
            dst_ref=dst.at[pl.ds(first, count)],
            send_sem=sems.at[at],
            recv_sem=sems.at[at + 1 + far],
            device_id=to,
            device_id_type=MESH,
        )

    def blk_send(src, dst, at):
        for y, z in offsets:
            tile = tile_of(y, z)
            blk_copy(src, dst, at, int(tile >= half_tiles), tile, 1, at_blk(y, z)).start()
        dst[own_tile] = src[own_tile]

    def blk_arrived(src, dst, at, far):
        count = half_tiles - 1 + far
        blk_copy(src, dst, at, far, far * half_tiles, count, at_blk(0, 1)).wait_recv()

    def blk_sent(src, dst, at):
        blk_copy(src, dst, at, 0, 0, blocks - 1, at_blk(0, 1)).wait_send()

    blk_send(out_a, in_a, 0)

    loads[3].wait()
    near = (near_v[...] - me * width + HALO) & (total - 1)
    near = jnp.where(
        near < HALO,
        near + width,
        jnp.where((near >= width) & (near < width + HALO), near - width, near),
    )
    wide = (width + 2 * HALO, width)
    spot = rows_of(wide)
    taps = jnp.where(spot == ((lanes_of(wide) + HALO) & (width - 1)), 1.0, 0.0)
    for index in range(4):
        taps = taps + jnp.where(spot == near[index : index + 1], 1.0, 0.0)
    taps = taps.astype(BF16)
    step = dot_nt(pick_lo[...], taps)
    step_lo[...] = step[:, :width].astype(BF16)
    halo_lo = step[:, width:]
    step = dot_nt(pick_hi[...], taps)
    step_hi[...] = step[:, :width].astype(BF16)
    step_halo[...] = jnp.concatenate([halo_lo, step[:, width:]], axis=1).astype(BF16)

    pltpu.make_async_copy(
        op_v.at[:, pl.ds(0, fields)], op_v.at[:, pl.ds(0, fields)], op_sem
    ).wait()
    depth = SIDE

    def spread(l, carry):
        block = op_v[l].astype(F32)
        block = jnp.where(
            lax.broadcasted_iota(I32, block.shape, 0) < fields, block, 0.0
        ).reshape(depth, block.shape[2])
        weight[pl.ds(pl.multiple_of(l * depth, depth), depth), :] = block.astype(BF16)
        return carry

    lax.fori_loop(0, levs, spread, 0)

    choose_row = rows_of((8, LANES))
    choose_lane = lanes_of((8, LANES))
    choose = jnp.zeros((8, LANES), F32)
    for at, lane in enumerate((56, 56 + SIDE, 58, 58 + SIDE)):
        here = choose_row == at
        choose = jnp.where(here & (choose_lane == lane), 32.0, choose)
        choose = jnp.where(here & (choose_lane == lane + 1), 1.0, choose)
    choose = choose.astype(BF16)

    def opened(buffer, far):
        stack = buffer[pl.ds(far * half_tiles, half_tiles)].astype(F32).reshape(half, LANES)
        return stack, both_sides(stack)

    slots = []
    edge = 2 * HALO

    def found(first, count, at, sides):
        target = ((rows_of((count, half)) + (first + width - HALO)) & (width - 1)) + 1
        return dot_nn(onehot(target == at[0:1]), sides[0]) + dot_nn(
            onehot(target == at[1:2]), sides[1]
        )

    blk_arrived(out_a, in_a, 0, 0)
    stack, sides = opened(in_a, 0)
    slots.append(dot_nt(choose, stack.astype(BF16)).astype(I32))
    partial[...] = found(0, width, slots[0], sides)

    blk_arrived(out_a, in_a, 0, 1)
    stack, sides = opened(in_a, 1)
    slots.append(dot_nt(choose, stack.astype(BF16)).astype(I32))
    cells[pl.ds(0, edge), :] = (partial[pl.ds(0, edge), :] + found(0, edge, slots[1], sides)).astype(BF16)

    up = pltpu.make_async_remote_copy(
        src_ref=cells.at[pl.ds(0, HALO)],
        dst_ref=halo.at[pl.ds(0, HALO)],
        send_sem=halo_sems.at[0],
        recv_sem=halo_sems.at[1],
        device_id=((me + 1) & (blocks - 1), my_lev),
        device_id_type=MESH,
    )
    down = pltpu.make_async_remote_copy(
        src_ref=cells.at[pl.ds(HALO, HALO)],
        dst_ref=halo.at[pl.ds(HALO, HALO)],
        send_sem=halo_sems.at[2],
        recv_sem=halo_sems.at[3],
        device_id=((me + blocks - 1) & (blocks - 1), my_lev),
        device_id_type=MESH,
    )
    up.start()
    down.start()

    if width > edge:
        rest = width - edge
        cells[pl.ds(edge, rest), :] = (
            partial[pl.ds(edge, rest), :] + found(edge, rest, slots[1], sides)
        ).astype(BF16)
    lo = dot_nn(step_lo[...], cells[...])
    hi = dot_nn(step_hi[...], cells[...])
    partial[...] = jnp.where(first_side, lo, hi)

    up.wait_recv()
    down.wait_recv()
    beside = halo[...]
    on_side = lanes_of(beside.shape) < SIDE
    none = jnp.zeros_like(beside)
    beside = jnp.concatenate(
        [jnp.where(on_side, beside, none), jnp.where(on_side, none, beside)], axis=0
    )
    summed = partial[...] + dot_nn(step_halo[...], beside)
    out_c[...] = (0.2 * summed).reshape(blocks, HALF, LANES).astype(BF16)
    blk_send(out_c, in_c, 3)

    per = levs * CAP
    line = rows_of((per, half))
    line = (line >> 4) * (2 * CAP) + (line & (CAP - 1)) + 1
    for far in range(2):
        span = slice(far * half, (far + 1) * half)
        place_lo[0:per, span] = onehot(line == slots[far][2:3])
        place_hi[0:per, span] = onehot(line == slots[far][3:4])
        place_lo[per : 2 * per, span] = onehot(line + CAP == slots[far][2:3])
        place_hi[per : 2 * per, span] = onehot(line + CAP == slots[far][3:4])

    blk_arrived(out_c, in_c, 3, 0)
    _, sides = opened(in_c, 0)
    partial[...] = dot_nn(place_lo[:, :half], sides[0]) + dot_nn(place_hi[:, :half], sides[1])
    blk_arrived(out_c, in_c, 3, 1)
    _, sides = opened(in_c, 1)
    placed = partial[...] + (
        dot_nn(place_lo[:, half:], sides[0]) + dot_nn(place_hi[:, half:], sides[1])
    )
    out_d[...] = (
        jnp.where(lanes_of((per, LANES)) < SIDE, placed[:per], placed[per:])
        .reshape(levs, CAP, LANES).astype(BF16)
    )

    for x, core in lev_offsets:
        to = at_lev(x, core)
        pltpu.make_async_remote_copy(
            src_ref=out_d.at[to],
            dst_ref=in_d.at[my_lev],
            send_sem=sems.at[6],
            recv_sem=lev_sems.at[x],
            device_id=(me, to),
            device_id_type=MESH,
        ).start()
    in_d[my_lev] = out_d[my_lev]

    def lev_wait(x, count):
        return pltpu.make_async_remote_copy(
            src_ref=out_d.at[pl.ds(0, count)],
            dst_ref=in_d.at[pl.ds(0, count)],
            send_sem=sems.at[6],
            recv_sem=lev_sems.at[x],
            device_id=(me, at_lev(0, 1)),
            device_id_type=MESH,
        )

    side = lanes_of((CAP, LANES)) < SIDE
    result = None
    for x in sorted(range(chips), key=lambda at: ring(at, chips)):
        lev_wait(x, 2 if x else 1).wait_recv()
        chip = ((my_lev >> 1) - x) & (chips - 1)
        even = in_d[2 * chip].astype(F32)
        odd = in_d[2 * chip + 1].astype(F32)
        upper = jnp.where(side, even, pltpu.roll(odd, SIDE, 1))
        lower = jnp.where(side, pltpu.roll(even, SIDE, 1), odd)
        columns = jnp.concatenate([upper, lower], axis=0).astype(BF16)
        term = dot_nn(columns, weight[pl.ds(pl.multiple_of(chip * LANES, LANES), LANES), :])
        result = term if result is None else result + term
    size = levs * lev_dev
    for field in range(fields):
        out_ref[field] = result[:, field * size : (field + 1) * size]

    blk_sent(out_a, in_a, 0)
    up.wait_send()
    down.wait_send()
    blk_sent(out_c, in_c, 3)
    lev_wait(0, levs - 1).wait_send()


def local(io_data, io_map, phys_map, neighbours, column_op):
    fields, lev_dev, width = io_data.shape
    blocks = lax.axis_size("blk")
    levs = lax.axis_size("lev")
    rows = blocks * HALF
    count = width // levs
    span = fields * levs * lev_dev
    any_space = pl.BlockSpec(memory_space=pl.ANY)
    result = pl.pallas_call(
        functools.partial(kernel, blocks, levs),
        out_shape=jax.ShapeDtypeStruct((fields, count, levs * lev_dev), F32),
        in_specs=[any_space] * 5,
        out_specs=pl.BlockSpec(memory_space=pltpu.VMEM),
        scratch_shapes=[
            pltpu.VMEM((fields, lev_dev, width), BF16),
            pltpu.VMEM((1, width), I32),
            pltpu.VMEM((1, width), I32),
            pltpu.VMEM((4, width), I32),
            pltpu.VMEM((levs, fields + 1, lev_dev, span), BF16),
            pltpu.VMEM((levs * SIDE, span), BF16),
            pltpu.VMEM((rows, width), BF16),
            pltpu.VMEM((rows, width), BF16),
            pltpu.VMEM((rows, width), BF16),
            pltpu.VMEM((rows, width), BF16),
            pltpu.VMEM((rows, 4 * HALO), BF16),
            pltpu.VMEM((width, rows), BF16),
            pltpu.VMEM((width, rows), BF16),
            pltpu.VMEM((width, LANES), BF16),
            pltpu.VMEM((2 * HALO, LANES), BF16),
            pltpu.VMEM((width, LANES), F32),
            pltpu.VMEM((blocks, HALF, LANES), BF16),
            pltpu.VMEM((blocks, HALF, LANES), BF16),
            pltpu.VMEM((blocks, HALF, LANES), BF16),
            pltpu.VMEM((blocks, HALF, LANES), BF16),
            pltpu.VMEM((levs, CAP, LANES), BF16),
            pltpu.VMEM((levs, CAP, LANES), BF16),
            pltpu.SemaphoreType.DMA((4,)),
            pltpu.SemaphoreType.DMA,
            pltpu.SemaphoreType.DMA((7,)),
            pltpu.SemaphoreType.DMA((4,)),
            pltpu.SemaphoreType.DMA((levs // 2,)),
        ],
        compiler_params=pltpu.CompilerParams(
            collective_id=0, has_side_effects=True, vmem_limit_bytes=60 * 1024 * 1024
        ),
    )(
        io_data,
        io_map.reshape(1, width),
        phys_map.reshape(1, width),
        neighbours,
        column_op.reshape(fields, levs, lev_dev, span),
    )
    return jnp.transpose(result, (1, 0, 2))


def solution(mesh):
    placed = (P(None, "lev", "blk"), P("blk"), P("blk"), P(None, "blk"), P())
    return jax.shard_map(
        local, mesh=mesh, in_specs=placed, out_specs=P(("blk", "lev"), None, None), check_vma=False
    )
```

```python
import functools

import jax
import jax.numpy as jnp
from jax import lax
from jax.experimental import pallas as pl
from jax.experimental.pallas import tpu as pltpu
from jax.sharding import PartitionSpec as P

HALO = 32
CAP = 16
HALF = CAP // 2
LANES = 128
SIDE = LANES // 2
MESH = pl.DeviceIdType.MESH
F32 = jnp.float32
BF16 = jnp.bfloat16
I32 = jnp.int32


def dot_nn(left, right):
    return lax.dot_general(left, right, (((1,), (0,)), ((), ())), preferred_element_type=F32)


def dot_nt(left, right):
    return lax.dot_general(left, right, (((1,), (1,)), ((), ())), preferred_element_type=F32)


def onehot(mask):
    return jnp.where(mask, 1.0, 0.0).astype(BF16)


def rows_of(shape):
    return lax.broadcasted_iota(I32, shape, 0)


def lanes_of(shape):
    return lax.broadcasted_iota(I32, shape, 1)


def both_sides(stack):
    turned = pltpu.roll(stack, SIDE, 1)
    first = lanes_of(stack.shape) < SIDE
    return jnp.where(first, stack, turned).astype(BF16), jnp.where(first, turned, stack).astype(BF16)


def ring(offset, count):
    return min(offset, count - offset)


def kernel(
    blocks, levs,
    io_hbm, io_map_hbm, phys_map_hbm, near_hbm, op_hbm,
    out_ref,
    io_v, io_map_v, phys_map_v, near_v, op_v, weight,
    pick_lo, pick_hi, step_lo, step_hi, step_halo, place_lo, place_hi, cells, halo, partial,
    out_a, mid_a, in_a, out_c, in_c, out_d, in_d,
    load_sem, op_sem, sems, row_sems, halo_sems, lev_sems, row_hello, column_hello, lev_hello,
):
    fields, lev_dev, width = io_v.shape
    rows = blocks * HALF
    total = blocks * width
    shift = width.bit_length() - 1
    me = lax.axis_index("blk")
    my_lev = lax.axis_index("lev")
    side_z = 1 << ((blocks.bit_length() - 1) // 2)
    side_y = blocks // side_z
    shift_z = side_z.bit_length() - 1
    my_y = me >> shift_z
    my_z = me & (side_z - 1)
    chips = levs // 2
    quarter = side_y // 4
    half_tiles = blocks // 2
    half = half_tiles * HALF
    offsets = sorted(
        ((y, z) for y in range(side_y) for z in range(side_z) if y or z),
        key=lambda at: (-ring(at[0], side_y) - ring(at[1], side_z), at),
    )
    lev_offsets = sorted(
        ((x, core) for x in range(chips) for core in range(2) if x or core),
        key=lambda at: (-ring(at[0], chips), at),
    )
    own_tile = quarter * side_z

    def tile_of(y, z):
        return ((y + quarter) % side_y) * side_z + z

    def at_blk(y, z):
        there = (((my_y + y) & (side_y - 1)) << shift_z) | ((my_z + z) & (side_z - 1))
        return there, my_lev

    def at_lev(x, core):
        return (((my_lev >> 1) + x) & (chips - 1)) * 2 + ((my_lev & 1) ^ core)

    def turn(at, count):
        return jnp.where(at < count // 2, at, count // 2 + count - 1 - at)

    row_turn = turn(my_y, side_y)
    lev_turn = turn(my_lev >> 1, chips) * 2 + (my_lev & 1)

    def turn_at_row(y):
        return turn((my_y + y) & (side_y - 1), side_y)

    def turn_at_lev(x, core):
        there = at_lev(x, core)
        return turn(there >> 1, chips) * 2 + (there & 1)

    far_rows = sorted(range(1, side_y), key=lambda at: -ring(at, side_y))
    far_columns = sorted(range(1, side_z), key=lambda at: -ring(at, side_z))

    loads = [
        pltpu.make_async_copy(src, dst, load_sem.at[at])
        for at, (src, dst) in enumerate(
            ((io_map_hbm, io_map_v), (phys_map_hbm, phys_map_v), (io_hbm, io_v), (near_hbm, near_v))
        )
    ]
    for load in loads:
        load.start()

    barrier = pltpu.get_barrier_semaphore()

    def greet(to, semaphore=barrier):
        pl.semaphore_signal(semaphore, inc=1, device_id=to, device_id_type=MESH)

    for y in far_rows:
        pl.when(turn_at_row(y) > row_turn)(functools.partial(greet, at_blk(y, 0)))
    for x, core in lev_offsets:
        pl.when(turn_at_lev(x, core) > lev_turn)(
            functools.partial(greet, (me, at_lev(x, core)))
        )
    for z in range(1, side_z):

        @pl.when(my_z + z < side_z)
        def _():
            for y in far_rows + [0]:
                greet(at_blk(y, z))

    def hear(semaphore, count):
        pl.when(count > 0)(functools.partial(pl.semaphore_wait, semaphore, count))

    hear(barrier, my_z * side_y + row_turn + lev_turn)
    for z in range(1, side_z):
        pl.when(my_z >= z)(functools.partial(greet, at_blk(0, -z), column_hello.at[z - 1]))
    for y in far_rows:
        pl.when(turn_at_row(y) < row_turn)(functools.partial(greet, at_blk(y, 0), row_hello))
    for x, core in lev_offsets:
        pl.when(turn_at_lev(x, core) < lev_turn)(
            functools.partial(greet, (me, at_lev(x, core)), lev_hello)
        )

    def load_op(l, carry):
        pltpu.make_async_copy(op_hbm.at[:, l], op_v.at[l, pl.ds(0, fields)], op_sem).start()
        return carry

    lax.fori_loop(0, levs, load_op, 0)

    before = onehot(rows_of((width, width)) < lanes_of((width, width)))
    loads[0].wait()
    loads[1].wait()
    codes = []
    members = []
    for ref in (io_map_v, phys_map_v):
        owner = ref[...] >> shift
        to_y = ((owner >> shift_z) - my_y + quarter) & (side_y - 1)
        to_z = ((owner & (side_z - 1)) - my_z) & (side_z - 1)
        tile = (to_y << shift_z) | to_z
        members.append((tile, rows_of((blocks, width)) == tile))
    ranked = dot_nn(
        jnp.concatenate([onehot(members[0][1]), onehot(members[1][1])], axis=0), before
    )
    for at, (tile, member) in enumerate(members):
        part = ranked[at * blocks : (at + 1) * blocks]
        rank = jnp.sum(jnp.where(member, part, 0.0), axis=0, keepdims=True).astype(I32)
        code = tile * HALF + rank
        codes.append(
            (jnp.where(rank < HALF, code, -1), jnp.where(rank >= HALF, code - HALF, -1))
        )

    loads[2].wait()
    meta_row = rows_of((8, width))

    def meta(ref, first):
        slot = (ref[...] & (width - 1)) + 1
        high = (slot >> 5).astype(F32)
        low = (slot & 31).astype(F32)
        return jnp.where(meta_row == first, high, jnp.where(meta_row == first + 1, low, 0.0))

    data = io_v[...].astype(F32).reshape(fields * lev_dev, width)
    one = jnp.concatenate([data, meta(io_map_v, 0)], axis=0)
    own = jnp.concatenate([one, one], axis=0).astype(BF16)
    one = jnp.concatenate([jnp.zeros_like(data), meta(phys_map_v, 2)], axis=0)
    later = jnp.concatenate([one, one], axis=0).astype(BF16)

    def slot_of(y):
        return (y + quarter) % side_y

    def tile_copy(y, z):
        return pltpu.make_async_remote_copy(
            src_ref=out_a.at[slot_of(y), z],
            dst_ref=in_a.at[slot_of(y), z],
            send_sem=sems.at[0 if z else 7],
            recv_sem=sems.at[1 if z else 8],
            device_id=at_blk(y, z),
            device_id_type=MESH,
        )

    first_side = lanes_of((rows, LANES)) < SIDE
    for far in (1, 0):
        where_row = rows_of((half, width)) + far * half
        here = pl.ds(far * half, half)
        pick_lo[here, :] = onehot(where_row == codes[1][0])
        pick_hi[here, :] = onehot(where_row == codes[1][1])
        lo = dot_nt(onehot(where_row == codes[0][0]), own) + dot_nt(pick_lo[here, :], later)
        hi = dot_nt(onehot(where_row == codes[0][1]), own) + dot_nt(pick_hi[here, :], later)
        out_a[pl.ds(far * (side_y // 2), side_y // 2)] = (
            jnp.where(first_side[:half], lo, hi)
            .reshape(side_y // 2, side_z, HALF, LANES).astype(BF16)
        )
        for z in far_columns:

            @pl.when(my_z + z >= side_z)
            def _():
                for y in far_rows + [0]:
                    if slot_of(y) // (side_y // 2) == far:
                        tile_copy(y, z).start()

    for y in far_rows:
        pl.when(turn_at_row(y) < row_turn)(tile_copy(y, 0).start)
    hear(row_hello, side_y - 1 - row_turn)
    for y in far_rows:
        pl.when(turn_at_row(y) > row_turn)(tile_copy(y, 0).start)

    def row_copy(first, count, z, to):
        return pltpu.make_async_remote_copy(
            src_ref=out_a.at[pl.ds(first, count), z],
            dst_ref=mid_a.at[pl.ds(first, count), z],
            send_sem=row_sems.at[z - 1, 0],
            recv_sem=row_sems.at[z - 1, 1],
            device_id=to,
            device_id_type=MESH,
        )

    for z in range(1, side_z):

        @pl.when(my_z + z < side_z)
        def _():
            for y in far_rows:
                row_copy(slot_of(y), 1, z, at_blk(y, 0)).start()

    mid_a[quarter] = out_a[quarter]
    in_a[quarter, 0] = out_a[quarter, 0]

    def blk_copy(src, dst, at, far, first, count, to):
        return pltpu.make_async_remote_copy(
            src_ref=src.at[pl.ds(first, count)],
            dst_ref=dst.at[pl.ds(first, count)],
            send_sem=sems.at[at],
            recv_sem=sems.at[at + 1 + far],
            device_id=to,
            device_id_type=MESH,
        )

    def blk_send(src, dst, at):
        for y, z in offsets:
            tile = tile_of(y, z)
            blk_copy(src, dst, at, int(tile >= half_tiles), tile, 1, at_blk(y, z)).start()
        dst[own_tile] = src[own_tile]

    def blk_arrived(src, dst, at, far):
        count = half_tiles - 1 + far
        blk_copy(src, dst, at, far, far * half_tiles, count, at_blk(0, 1)).wait_recv()

    def blk_sent(src, dst, at):
        blk_copy(src, dst, at, 0, 0, blocks - 1, at_blk(0, 1)).wait_send()

    loads[3].wait()
    near = (near_v[...] - me * width + HALO) & (total - 1)
    near = jnp.where(
        near < HALO,
        near + width,
        jnp.where((near >= width) & (near < width + HALO), near - width, near),
    )
    wide = (width + 2 * HALO, width)
    spot = rows_of(wide)
    taps = jnp.where(spot == ((lanes_of(wide) + HALO) & (width - 1)), 1.0, 0.0)
    for index in range(4):
        taps = taps + jnp.where(spot == near[index : index + 1], 1.0, 0.0)
    taps = taps.astype(BF16)
    step = dot_nt(pick_lo[...], taps)
    step_lo[...] = step[:, :width].astype(BF16)
    halo_lo = step[:, width:]
    step = dot_nt(pick_hi[...], taps)
    step_hi[...] = step[:, :width].astype(BF16)
    step_halo[...] = jnp.concatenate([halo_lo, step[:, width:]], axis=1).astype(BF16)

    pltpu.make_async_copy(
        op_v.at[:, pl.ds(0, fields)], op_v.at[:, pl.ds(0, fields)], op_sem
    ).wait()
    depth = SIDE

    def spread(l, carry):
        block = op_v[l].astype(F32)
        block = jnp.where(
            lax.broadcasted_iota(I32, block.shape, 0) < fields, block, 0.0
        ).reshape(depth, block.shape[2])
        weight[pl.ds(pl.multiple_of(l * depth, depth), depth), :] = block.astype(BF16)
        return carry

    lax.fori_loop(0, levs, spread, 0)

    choose_row = rows_of((8, LANES))
    choose_lane = lanes_of((8, LANES))
    choose = jnp.zeros((8, LANES), F32)
    for at, lane in enumerate((56, 56 + SIDE, 58, 58 + SIDE)):
        here = choose_row == at
        choose = jnp.where(here & (choose_lane == lane), 32.0, choose)
        choose = jnp.where(here & (choose_lane == lane + 1), 1.0, choose)
    choose = choose.astype(BF16)

    def column_copy(first, count, z):
        return pltpu.make_async_remote_copy(
            src_ref=mid_a.at[:, pl.ds(first, count)],
            dst_ref=in_a.at[:, pl.ds(first, count)],
            send_sem=sems.at[0],
            recv_sem=sems.at[1],
            device_id=at_blk(0, z),
            device_id_type=MESH,
        )

    for z in range(1, side_z):

        @pl.when(my_z + z < side_z)
        def _():
            row_copy(0, side_y - 1, z, at_blk(1, 0)).wait_recv()
            pl.semaphore_wait(column_hello.at[z - 1], 1)
            column_copy(z, 1, z).start()

    row_tiles = pltpu.make_async_remote_copy(
        src_ref=out_a.at[pl.ds(0, side_y - 1), 0],
        dst_ref=in_a.at[pl.ds(0, side_y - 1), 0],
        send_sem=sems.at[7],
        recv_sem=sems.at[8],
        device_id=at_blk(1, 0),
        device_id_type=MESH,
    )

    edge = 2 * HALO
    row_tiles.wait_recv()
    column_copy(1, side_z - 1, 1).wait_recv()
    stack = in_a[...].astype(F32).reshape(rows, LANES)
    sides = both_sides(stack)
    slots = dot_nt(choose, stack.astype(BF16)).astype(I32)

    def found(first, count):
        target = ((rows_of((count, rows)) + (first + width - HALO)) & (width - 1)) + 1
        return (
            dot_nn(onehot(target == slots[0:1]), sides[0])
            + dot_nn(onehot(target == slots[1:2]), sides[1])
        ).astype(BF16)

    cells[pl.ds(0, edge), :] = found(0, edge)

    up = pltpu.make_async_remote_copy(
        src_ref=cells.at[pl.ds(0, HALO)],
        dst_ref=halo.at[pl.ds(0, HALO)],
        send_sem=halo_sems.at[0],
        recv_sem=halo_sems.at[1],
        device_id=((me + 1) & (blocks - 1), my_lev),
        device_id_type=MESH,
    )
    down = pltpu.make_async_remote_copy(
        src_ref=cells.at[pl.ds(HALO, HALO)],
        dst_ref=halo.at[pl.ds(HALO, HALO)],
        send_sem=halo_sems.at[2],
        recv_sem=halo_sems.at[3],
        device_id=((me + blocks - 1) & (blocks - 1), my_lev),
        device_id_type=MESH,
    )
    up.start()
    down.start()

    if width > edge:
        rest = width - edge
        cells[pl.ds(edge, rest), :] = found(edge, rest)
    lo = dot_nn(step_lo[...], cells[...])
    hi = dot_nn(step_hi[...], cells[...])
    partial[...] = jnp.where(first_side, lo, hi)

    up.wait_recv()
    down.wait_recv()
    beside = halo[...]
    on_side = lanes_of(beside.shape) < SIDE
    none = jnp.zeros_like(beside)
    beside = jnp.concatenate(
        [jnp.where(on_side, beside, none), jnp.where(on_side, none, beside)], axis=0
    )
    summed = partial[...] + dot_nn(step_halo[...], beside)
    out_c[...] = (0.2 * summed).reshape(blocks, HALF, LANES).astype(BF16)
    blk_send(out_c, in_c, 3)

    per = levs * CAP
    line = rows_of((per, rows))
    line = (line >> 4) * (2 * CAP) + (line & (CAP - 1)) + 1
    place_lo[0:per, :] = onehot(line == slots[2:3])
    place_hi[0:per, :] = onehot(line == slots[3:4])
    place_lo[per : 2 * per, :] = onehot(line + CAP == slots[2:3])
    place_hi[per : 2 * per, :] = onehot(line + CAP == slots[3:4])

    def opened(buffer, far):
        stack = buffer[pl.ds(far * half_tiles, half_tiles)].astype(F32).reshape(half, LANES)
        return both_sides(stack)

    blk_arrived(out_c, in_c, 3, 0)
    sides = opened(in_c, 0)
    partial[...] = dot_nn(place_lo[:, :half], sides[0]) + dot_nn(place_hi[:, :half], sides[1])
    blk_arrived(out_c, in_c, 3, 1)
    sides = opened(in_c, 1)
    placed = partial[...] + (
        dot_nn(place_lo[:, half:], sides[0]) + dot_nn(place_hi[:, half:], sides[1])
    )
    out_d[...] = (
        jnp.where(lanes_of((per, LANES)) < SIDE, placed[:per], placed[per:])
        .reshape(levs, CAP, LANES).astype(BF16)
    )

    hear(lev_hello, levs - 1 - lev_turn)
    for x, core in lev_offsets:
        to = at_lev(x, core)
        pltpu.make_async_remote_copy(
            src_ref=out_d.at[to],
            dst_ref=in_d.at[my_lev],
            send_sem=sems.at[6],
            recv_sem=lev_sems.at[x],
            device_id=(me, to),
            device_id_type=MESH,
        ).start()
    in_d[my_lev] = out_d[my_lev]

    def lev_wait(x, count):
        return pltpu.make_async_remote_copy(
            src_ref=out_d.at[pl.ds(0, count)],
            dst_ref=in_d.at[pl.ds(0, count)],
            send_sem=sems.at[6],
            recv_sem=lev_sems.at[x],
            device_id=(me, at_lev(0, 1)),
            device_id_type=MESH,
        )

    side = lanes_of((CAP, LANES)) < SIDE
    result = None
    for x in sorted(range(chips), key=lambda at: ring(at, chips)):
        lev_wait(x, 2 if x else 1).wait_recv()
        chip = ((my_lev >> 1) - x) & (chips - 1)
        even = in_d[2 * chip].astype(F32)
        odd = in_d[2 * chip + 1].astype(F32)
        upper = jnp.where(side, even, pltpu.roll(odd, SIDE, 1))
        lower = jnp.where(side, pltpu.roll(even, SIDE, 1), odd)
        columns = jnp.concatenate([upper, lower], axis=0).astype(BF16)
        term = dot_nn(columns, weight[pl.ds(pl.multiple_of(chip * LANES, LANES), LANES), :])
        result = term if result is None else result + term
    size = levs * lev_dev
    for field in range(fields):
        out_ref[field] = result[:, field * size : (field + 1) * size]

    row_tiles.wait_send()
    column_copy(1, side_z - 1, 1).wait_send()
    for z in range(1, side_z):
        pl.when(my_z + z < side_z)(row_copy(0, side_y - 1, z, at_blk(1, 0)).wait_send)
    up.wait_send()
    down.wait_send()
    blk_sent(out_c, in_c, 3)
    lev_wait(0, levs - 1).wait_send()


def local(io_data, io_map, phys_map, neighbours, column_op):
    fields, lev_dev, width = io_data.shape
    blocks = lax.axis_size("blk")
    levs = lax.axis_size("lev")
    rows = blocks * HALF
    count = width // levs
    span = fields * levs * lev_dev
    side_z = 1 << ((blocks.bit_length() - 1) // 2)
    side_y = blocks // side_z
    any_space = pl.BlockSpec(memory_space=pl.ANY)
    result = pl.pallas_call(
        functools.partial(kernel, blocks, levs),
        out_shape=jax.ShapeDtypeStruct((fields, count, levs * lev_dev), F32),
        in_specs=[any_space] * 5,
        out_specs=pl.BlockSpec(memory_space=pltpu.VMEM),
        scratch_shapes=[
            pltpu.VMEM((fields, lev_dev, width), BF16),
            pltpu.VMEM((1, width), I32),
            pltpu.VMEM((1, width), I32),
            pltpu.VMEM((4, width), I32),
            pltpu.VMEM((levs, fields + 1, lev_dev, span), BF16),
            pltpu.VMEM((levs * SIDE, span), BF16),
            pltpu.VMEM((rows, width), BF16),
            pltpu.VMEM((rows, width), BF16),
            pltpu.VMEM((rows, width), BF16),
            pltpu.VMEM((rows, width), BF16),
            pltpu.VMEM((rows, 4 * HALO), BF16),
            pltpu.VMEM((width, rows), BF16),
            pltpu.VMEM((width, rows), BF16),
            pltpu.VMEM((width, LANES), BF16),
            pltpu.VMEM((2 * HALO, LANES), BF16),
            pltpu.VMEM((width, LANES), F32),
            pltpu.VMEM((side_y, side_z, HALF, LANES), BF16),
            pltpu.VMEM((side_y, side_z, HALF, LANES), BF16),
            pltpu.VMEM((side_y, side_z, HALF, LANES), BF16),
            pltpu.VMEM((blocks, HALF, LANES), BF16),
            pltpu.VMEM((blocks, HALF, LANES), BF16),
            pltpu.VMEM((levs, CAP, LANES), BF16),
            pltpu.VMEM((levs, CAP, LANES), BF16),
            pltpu.SemaphoreType.DMA((4,)),
            pltpu.SemaphoreType.DMA,
            pltpu.SemaphoreType.DMA((9,)),
            pltpu.SemaphoreType.DMA((side_z - 1, 2)),
            pltpu.SemaphoreType.DMA((4,)),
            pltpu.SemaphoreType.DMA((levs // 2,)),
            pltpu.SemaphoreType.REGULAR,
            pltpu.SemaphoreType.REGULAR((side_z - 1,)),
            pltpu.SemaphoreType.REGULAR,
        ],
        compiler_params=pltpu.CompilerParams(
            collective_id=0, has_side_effects=True, vmem_limit_bytes=60 * 1024 * 1024
        ),
    )(
        io_data,
        io_map.reshape(1, width),
        phys_map.reshape(1, width),
        neighbours,
        column_op.reshape(fields, levs, lev_dev, span),
    )
    return jnp.transpose(result, (1, 0, 2))


def solution(mesh):
    placed = (P(None, "lev", "blk"), P("blk"), P("blk"), P(None, "blk"), P())
    return jax.shard_map(
        local, mesh=mesh, in_specs=placed, out_specs=P(("blk", "lev"), None, None), check_vma=False
    )
```

```python
import functools

import jax
import jax.numpy as jnp
from jax import lax
from jax.experimental import pallas as pl
from jax.experimental.pallas import tpu as pltpu
from jax.sharding import PartitionSpec as P

HALO = 32
CAP = 16
HALF = CAP // 2
LANES = 128
SIDE = LANES // 2
MESH = pl.DeviceIdType.MESH
F32 = jnp.float32
BF16 = jnp.bfloat16
I32 = jnp.int32


def dot_nn(left, right):
    return lax.dot_general(left, right, (((1,), (0,)), ((), ())), preferred_element_type=F32)


def dot_nt(left, right):
    return lax.dot_general(left, right, (((1,), (1,)), ((), ())), preferred_element_type=F32)


def onehot(mask):
    return jnp.where(mask, 1.0, 0.0).astype(BF16)


def rows_of(shape):
    return lax.broadcasted_iota(I32, shape, 0)


def lanes_of(shape):
    return lax.broadcasted_iota(I32, shape, 1)


def both_sides(stack):
    turned = pltpu.roll(stack, SIDE, 1)
    first = lanes_of(stack.shape) < SIDE
    return jnp.where(first, stack, turned).astype(BF16), jnp.where(first, turned, stack).astype(BF16)


def ring(offset, count):
    return min(offset, count - offset)


def kernel(
    blocks, levs,
    io_hbm, io_map_hbm, phys_map_hbm, near_hbm, op_hbm,
    out_ref,
    io_v, io_map_v, phys_map_v, near_v, op_v, weight,
    pick_lo, pick_hi, step_lo, step_hi, step_halo, place_lo, place_hi, cells, halo, partial,
    out_a, mid_a, in_a, out_c, in_c, out_d, in_d,
    load_sem, op_sem, sems, row_sems, halo_sems, lev_sems, row_hello, column_hello, lev_hello,
):
    fields, lev_dev, width = io_v.shape
    rows = blocks * HALF
    total = blocks * width
    shift = width.bit_length() - 1
    me = lax.axis_index("blk")
    my_lev = lax.axis_index("lev")
    side_z = 1 << ((blocks.bit_length() - 1) // 2)
    side_y = blocks // side_z
    shift_z = side_z.bit_length() - 1
    my_y = me >> shift_z
    my_z = me & (side_z - 1)
    chips = levs // 2
    quarter = side_y // 4
    half_tiles = blocks // 2
    half = half_tiles * HALF
    offsets = sorted(
        ((y, z) for y in range(side_y) for z in range(side_z) if y or z),
        key=lambda at: (-ring(at[0], side_y) - ring(at[1], side_z), at),
    )
    lev_offsets = sorted(
        ((x, core) for x in range(chips) for core in range(2) if x or core),
        key=lambda at: (-ring(at[0], chips), at),
    )
    own_tile = quarter * side_z

    def tile_of(y, z):
        return ((y + quarter) % side_y) * side_z + z

    def at_blk(y, z):
        there = (((my_y + y) & (side_y - 1)) << shift_z) | ((my_z + z) & (side_z - 1))
        return there, my_lev

    def at_lev(x, core):
        return (((my_lev >> 1) + x) & (chips - 1)) * 2 + ((my_lev & 1) ^ core)

    def turn(at, count):
        return jnp.where(at < count // 2, at, count // 2 + count - 1 - at)

    row_turn = turn(my_y, side_y)
    lev_turn = turn(my_lev >> 1, chips) * 2 + (my_lev & 1)

    def turn_at_row(y):
        return turn((my_y + y) & (side_y - 1), side_y)

    def turn_at_lev(x, core):
        there = at_lev(x, core)
        return turn(there >> 1, chips) * 2 + (there & 1)

    far_rows = sorted(range(1, side_y), key=lambda at: -ring(at, side_y))
    far_columns = sorted(range(1, side_z), key=lambda at: -ring(at, side_z))

    loads = [
        pltpu.make_async_copy(src, dst, load_sem.at[at])
        for at, (src, dst) in enumerate(
            ((io_map_hbm, io_map_v), (phys_map_hbm, phys_map_v), (io_hbm, io_v), (near_hbm, near_v))
        )
    ]
    for load in loads:
        load.start()

    barrier = pltpu.get_barrier_semaphore()

    def greet(to, semaphore=barrier):
        pl.semaphore_signal(semaphore, inc=1, device_id=to, device_id_type=MESH)

    for y in far_rows:
        pl.when(turn_at_row(y) > row_turn)(functools.partial(greet, at_blk(y, 0)))
    for x, core in lev_offsets:
        pl.when(turn_at_lev(x, core) > lev_turn)(
            functools.partial(greet, (me, at_lev(x, core)))
        )
    for z in range(1, side_z):

        @pl.when(my_z + z < side_z)
        def _():
            for y in far_rows + [0]:
                greet(at_blk(y, z))

    def hear(semaphore, count):
        pl.when(count > 0)(functools.partial(pl.semaphore_wait, semaphore, count))

    hear(barrier, my_z * side_y + row_turn + lev_turn)
    for z in range(1, side_z):
        pl.when(my_z >= z)(functools.partial(greet, at_blk(0, -z), column_hello.at[z - 1]))
    for y in far_rows:
        pl.when(turn_at_row(y) < row_turn)(functools.partial(greet, at_blk(y, 0), row_hello))

    before = onehot(rows_of((width, width)) < lanes_of((width, width)))
    loads[0].wait()
    loads[1].wait()
    codes = []
    members = []
    for ref in (io_map_v, phys_map_v):
        owner = ref[...] >> shift
        to_y = ((owner >> shift_z) - my_y + quarter) & (side_y - 1)
        to_z = ((owner & (side_z - 1)) - my_z) & (side_z - 1)
        tile = (to_y << shift_z) | to_z
        members.append((tile, rows_of((blocks, width)) == tile))
    ranked = dot_nn(
        jnp.concatenate([onehot(members[0][1]), onehot(members[1][1])], axis=0), before
    )
    for at, (tile, member) in enumerate(members):
        part = ranked[at * blocks : (at + 1) * blocks]
        rank = jnp.sum(jnp.where(member, part, 0.0), axis=0, keepdims=True).astype(I32)
        code = tile * HALF + rank
        codes.append(
            (jnp.where(rank < HALF, code, -1), jnp.where(rank >= HALF, code - HALF, -1))
        )

    loads[2].wait()
    meta_row = rows_of((8, width))

    def meta(ref, first):
        slot = (ref[...] & (width - 1)) + 1
        high = (slot >> 5).astype(F32)
        low = (slot & 31).astype(F32)
        return jnp.where(meta_row == first, high, jnp.where(meta_row == first + 1, low, 0.0))

    data = io_v[...].astype(F32).reshape(fields * lev_dev, width)
    one = jnp.concatenate([data, meta(io_map_v, 0)], axis=0)
    own = jnp.concatenate([one, one], axis=0).astype(BF16)
    one = jnp.concatenate([jnp.zeros_like(data), meta(phys_map_v, 2)], axis=0)
    later = jnp.concatenate([one, one], axis=0).astype(BF16)

    def slot_of(y):
        return (y + quarter) % side_y

    def tile_copy(y, z):
        return pltpu.make_async_remote_copy(
            src_ref=out_a.at[slot_of(y), z],
            dst_ref=in_a.at[slot_of(y), z],
            send_sem=sems.at[0 if z else 7],
            recv_sem=sems.at[1 if z else 8],
            device_id=at_blk(y, z),
            device_id_type=MESH,
        )

    first_side = lanes_of((rows, LANES)) < SIDE
    for far in (1, 0):
        where_row = rows_of((half, width)) + far * half
        here = pl.ds(far * half, half)
        pick_lo[here, :] = onehot(where_row == codes[1][0])
        pick_hi[here, :] = onehot(where_row == codes[1][1])
        lo = dot_nt(onehot(where_row == codes[0][0]), own) + dot_nt(pick_lo[here, :], later)
        hi = dot_nt(onehot(where_row == codes[0][1]), own) + dot_nt(pick_hi[here, :], later)
        out_a[pl.ds(far * (side_y // 2), side_y // 2)] = (
            jnp.where(first_side[:half], lo, hi)
            .reshape(side_y // 2, side_z, HALF, LANES).astype(BF16)
        )
        for z in far_columns:

            @pl.when(my_z + z >= side_z)
            def _():
                for y in far_rows + [0]:
                    if slot_of(y) // (side_y // 2) == far:
                        tile_copy(y, z).start()

    for y in far_rows:
        pl.when(turn_at_row(y) < row_turn)(tile_copy(y, 0).start)
    hear(row_hello, side_y - 1 - row_turn)
    for y in far_rows:
        pl.when(turn_at_row(y) > row_turn)(tile_copy(y, 0).start)

    def row_copy(first, count, z, to):
        return pltpu.make_async_remote_copy(
            src_ref=out_a.at[pl.ds(first, count), z],
            dst_ref=mid_a.at[pl.ds(first, count), z],
            send_sem=row_sems.at[z - 1, 0],
            recv_sem=row_sems.at[z - 1, 1],
            device_id=to,
            device_id_type=MESH,
        )

    for z in range(1, side_z):

        @pl.when(my_z + z < side_z)
        def _():
            for y in far_rows:
                row_copy(slot_of(y), 1, z, at_blk(y, 0)).start()

    mid_a[quarter] = out_a[quarter]
    in_a[quarter, 0] = out_a[quarter, 0]

    for x, core in lev_offsets:
        pl.when(turn_at_lev(x, core) < lev_turn)(
            functools.partial(greet, (me, at_lev(x, core)), lev_hello)
        )

    def load_op(l, carry):
        pltpu.make_async_copy(op_hbm.at[:, l], op_v.at[l, pl.ds(0, fields)], op_sem).start()
        return carry

    lax.fori_loop(0, levs, load_op, 0)

    def blk_copy(src, dst, at, far, first, count, to):
        return pltpu.make_async_remote_copy(
            src_ref=src.at[pl.ds(first, count)],
            dst_ref=dst.at[pl.ds(first, count)],
            send_sem=sems.at[at],
            recv_sem=sems.at[at + 1 + far],
            device_id=to,
            device_id_type=MESH,
        )

    def blk_send(src, dst, at, far):
        for y, z in offsets:
            tile = tile_of(y, z)
            if tile // half_tiles == far:
                blk_copy(src, dst, at, far, tile, 1, at_blk(y, z)).start()

    def blk_arrived(src, dst, at, far):
        count = half_tiles - 1 + far
        blk_copy(src, dst, at, far, far * half_tiles, count, at_blk(0, 1)).wait_recv()

    def blk_sent(src, dst, at):
        blk_copy(src, dst, at, 0, 0, blocks - 1, at_blk(0, 1)).wait_send()

    loads[3].wait()
    near = (near_v[...] - me * width + HALO) & (total - 1)
    near = jnp.where(
        near < HALO,
        near + width,
        jnp.where((near >= width) & (near < width + HALO), near - width, near),
    )
    wide = (width + 2 * HALO, width)
    spot = rows_of(wide)
    taps = jnp.where(spot == ((lanes_of(wide) + HALO) & (width - 1)), 1.0, 0.0)
    for index in range(4):
        taps = taps + jnp.where(spot == near[index : index + 1], 1.0, 0.0)
    taps = taps.astype(BF16)
    step = dot_nt(pick_lo[...], taps)
    step_lo[...] = step[:, :width].astype(BF16)
    halo_lo = step[:, width:]
    step = dot_nt(pick_hi[...], taps)
    step_hi[...] = step[:, :width].astype(BF16)
    step_halo[...] = jnp.concatenate([halo_lo, step[:, width:]], axis=1).astype(BF16)

    pltpu.make_async_copy(
        op_v.at[:, pl.ds(0, fields)], op_v.at[:, pl.ds(0, fields)], op_sem
    ).wait()
    depth = SIDE

    def spread(l, carry):
        block = op_v[l].astype(F32)
        block = jnp.where(
            lax.broadcasted_iota(I32, block.shape, 0) < fields, block, 0.0
        ).reshape(depth, block.shape[2])
        weight[pl.ds(pl.multiple_of(l * depth, depth), depth), :] = block.astype(BF16)
        return carry

    lax.fori_loop(0, levs, spread, 0)

    choose_row = rows_of((8, LANES))
    choose_lane = lanes_of((8, LANES))
    choose = jnp.zeros((8, LANES), F32)
    for at, lane in enumerate((56, 56 + SIDE, 58, 58 + SIDE)):
        here = choose_row == at
        choose = jnp.where(here & (choose_lane == lane), 32.0, choose)
        choose = jnp.where(here & (choose_lane == lane + 1), 1.0, choose)
    choose = choose.astype(BF16)

    def column_copy(first, count, z):
        return pltpu.make_async_remote_copy(
            src_ref=mid_a.at[:, pl.ds(first, count)],
            dst_ref=in_a.at[:, pl.ds(first, count)],
            send_sem=sems.at[0],
            recv_sem=sems.at[1],
            device_id=at_blk(0, z),
            device_id_type=MESH,
        )

    for z in range(1, side_z):

        @pl.when(my_z + z < side_z)
        def _():
            row_copy(0, side_y - 1, z, at_blk(1, 0)).wait_recv()
            pl.semaphore_wait(column_hello.at[z - 1], 1)
            column_copy(z, 1, z).start()

    row_tiles = pltpu.make_async_remote_copy(
        src_ref=out_a.at[pl.ds(0, side_y - 1), 0],
        dst_ref=in_a.at[pl.ds(0, side_y - 1), 0],
        send_sem=sems.at[7],
        recv_sem=sems.at[8],
        device_id=at_blk(1, 0),
        device_id_type=MESH,
    )

    edge = 2 * HALO
    row_tiles.wait_recv()
    column_copy(1, side_z - 1, 1).wait_recv()
    stack = in_a[...].astype(F32).reshape(rows, LANES)
    sides = both_sides(stack)
    slots = dot_nt(choose, stack.astype(BF16)).astype(I32)

    def found(first, count):
        target = ((rows_of((count, rows)) + (first + width - HALO)) & (width - 1)) + 1
        return (
            dot_nn(onehot(target == slots[0:1]), sides[0])
            + dot_nn(onehot(target == slots[1:2]), sides[1])
        ).astype(BF16)

    cells[pl.ds(0, edge), :] = found(0, edge)

    up = pltpu.make_async_remote_copy(
        src_ref=cells.at[pl.ds(0, HALO)],
        dst_ref=halo.at[pl.ds(0, HALO)],
        send_sem=halo_sems.at[0],
        recv_sem=halo_sems.at[1],
        device_id=((me + 1) & (blocks - 1), my_lev),
        device_id_type=MESH,
    )
    down = pltpu.make_async_remote_copy(
        src_ref=cells.at[pl.ds(HALO, HALO)],
        dst_ref=halo.at[pl.ds(HALO, HALO)],
        send_sem=halo_sems.at[2],
        recv_sem=halo_sems.at[3],
        device_id=((me + blocks - 1) & (blocks - 1), my_lev),
        device_id_type=MESH,
    )
    up.start()
    down.start()

    if width > edge:
        rest = width - edge
        cells[pl.ds(edge, rest), :] = found(edge, rest)
    lo = dot_nn(step_lo[...], cells[...])
    hi = dot_nn(step_hi[...], cells[...])
    partial[...] = jnp.where(first_side, lo, hi)

    up.wait_recv()
    down.wait_recv()
    beside = halo[...]
    on_side = lanes_of(beside.shape) < SIDE
    none = jnp.zeros_like(beside)
    beside = jnp.concatenate(
        [jnp.where(on_side, beside, none), jnp.where(on_side, none, beside)], axis=0
    )
    for far in (1, 0):
        here = pl.ds(far * half, half)
        summed = partial[here, :] + dot_nn(step_halo[here, :], beside)
        out_c[pl.ds(far * half_tiles, half_tiles)] = (
            (0.2 * summed).reshape(half_tiles, HALF, LANES).astype(BF16)
        )
        blk_send(out_c, in_c, 3, far)
    in_c[own_tile] = out_c[own_tile]

    per = levs * CAP
    line = rows_of((per, rows))
    line = (line >> 4) * (2 * CAP) + (line & (CAP - 1)) + 1
    place_lo[0:per, :] = onehot(line == slots[2:3])
    place_hi[0:per, :] = onehot(line == slots[3:4])
    place_lo[per : 2 * per, :] = onehot(line + CAP == slots[2:3])
    place_hi[per : 2 * per, :] = onehot(line + CAP == slots[3:4])

    def opened(buffer, far):
        stack = buffer[pl.ds(far * half_tiles, half_tiles)].astype(F32).reshape(half, LANES)
        return both_sides(stack)

    blk_arrived(out_c, in_c, 3, 0)
    sides = opened(in_c, 0)
    partial[...] = dot_nn(place_lo[:, :half], sides[0]) + dot_nn(place_hi[:, :half], sides[1])
    blk_arrived(out_c, in_c, 3, 1)
    sides = opened(in_c, 1)
    placed = partial[...] + (
        dot_nn(place_lo[:, half:], sides[0]) + dot_nn(place_hi[:, half:], sides[1])
    )
    out_d[...] = (
        jnp.where(lanes_of((per, LANES)) < SIDE, placed[:per], placed[per:])
        .reshape(levs, CAP, LANES).astype(BF16)
    )

    hear(lev_hello, levs - 1 - lev_turn)
    for x, core in lev_offsets:
        to = at_lev(x, core)
        pltpu.make_async_remote_copy(
            src_ref=out_d.at[to],
            dst_ref=in_d.at[my_lev],
            send_sem=sems.at[6],
            recv_sem=lev_sems.at[x],
            device_id=(me, to),
            device_id_type=MESH,
        ).start()
    in_d[my_lev] = out_d[my_lev]

    def lev_wait(x, count):
        return pltpu.make_async_remote_copy(
            src_ref=out_d.at[pl.ds(0, count)],
            dst_ref=in_d.at[pl.ds(0, count)],
            send_sem=sems.at[6],
            recv_sem=lev_sems.at[x],
            device_id=(me, at_lev(0, 1)),
            device_id_type=MESH,
        )

    side = lanes_of((CAP, LANES)) < SIDE
    result = None
    for x in sorted(range(chips), key=lambda at: ring(at, chips)):
        lev_wait(x, 2 if x else 1).wait_recv()
        chip = ((my_lev >> 1) - x) & (chips - 1)
        even = in_d[2 * chip].astype(F32)
        odd = in_d[2 * chip + 1].astype(F32)
        upper = jnp.where(side, even, pltpu.roll(odd, SIDE, 1))
        lower = jnp.where(side, pltpu.roll(even, SIDE, 1), odd)
        columns = jnp.concatenate([upper, lower], axis=0).astype(BF16)
        term = dot_nn(columns, weight[pl.ds(pl.multiple_of(chip * LANES, LANES), LANES), :])
        result = term if result is None else result + term
    size = levs * lev_dev
    for field in range(fields):
        out_ref[field] = result[:, field * size : (field + 1) * size]

    row_tiles.wait_send()
    column_copy(1, side_z - 1, 1).wait_send()
    for z in range(1, side_z):
        pl.when(my_z + z < side_z)(row_copy(0, side_y - 1, z, at_blk(1, 0)).wait_send)
    up.wait_send()
    down.wait_send()
    blk_sent(out_c, in_c, 3)
    lev_wait(0, levs - 1).wait_send()


def local(io_data, io_map, phys_map, neighbours, column_op):
    fields, lev_dev, width = io_data.shape
    blocks = lax.axis_size("blk")
    levs = lax.axis_size("lev")
    rows = blocks * HALF
    count = width // levs
    span = fields * levs * lev_dev
    side_z = 1 << ((blocks.bit_length() - 1) // 2)
    side_y = blocks // side_z
    any_space = pl.BlockSpec(memory_space=pl.ANY)
    result = pl.pallas_call(
        functools.partial(kernel, blocks, levs),
        out_shape=jax.ShapeDtypeStruct((fields, count, levs * lev_dev), F32),
        in_specs=[any_space] * 5,
        out_specs=pl.BlockSpec(memory_space=pltpu.VMEM),
        scratch_shapes=[
            pltpu.VMEM((fields, lev_dev, width), BF16),
            pltpu.VMEM((1, width), I32),
            pltpu.VMEM((1, width), I32),
            pltpu.VMEM((4, width), I32),
            pltpu.VMEM((levs, fields + 1, lev_dev, span), BF16),
            pltpu.VMEM((levs * SIDE, span), BF16),
            pltpu.VMEM((rows, width), BF16),
            pltpu.VMEM((rows, width), BF16),
            pltpu.VMEM((rows, width), BF16),
            pltpu.VMEM((rows, width), BF16),
            pltpu.VMEM((rows, 4 * HALO), BF16),
            pltpu.VMEM((width, rows), BF16),
            pltpu.VMEM((width, rows), BF16),
            pltpu.VMEM((width, LANES), BF16),
            pltpu.VMEM((2 * HALO, LANES), BF16),
            pltpu.VMEM((width, LANES), F32),
            pltpu.VMEM((side_y, side_z, HALF, LANES), BF16),
            pltpu.VMEM((side_y, side_z, HALF, LANES), BF16),
            pltpu.VMEM((side_y, side_z, HALF, LANES), BF16),
            pltpu.VMEM((blocks, HALF, LANES), BF16),
            pltpu.VMEM((blocks, HALF, LANES), BF16),
            pltpu.VMEM((levs, CAP, LANES), BF16),
            pltpu.VMEM((levs, CAP, LANES), BF16),
            pltpu.SemaphoreType.DMA((4,)),
            pltpu.SemaphoreType.DMA,
            pltpu.SemaphoreType.DMA((9,)),
            pltpu.SemaphoreType.DMA((side_z - 1, 2)),
            pltpu.SemaphoreType.DMA((4,)),
            pltpu.SemaphoreType.DMA((levs // 2,)),
            pltpu.SemaphoreType.REGULAR,
            pltpu.SemaphoreType.REGULAR((side_z - 1,)),
            pltpu.SemaphoreType.REGULAR,
        ],
        compiler_params=pltpu.CompilerParams(
            collective_id=0, has_side_effects=True, vmem_limit_bytes=60 * 1024 * 1024
        ),
    )(
        io_data,
        io_map.reshape(1, width),
        phys_map.reshape(1, width),
        neighbours,
        column_op.reshape(fields, levs, lev_dev, span),
    )
    return jnp.transpose(result, (1, 0, 2))


def solution(mesh):
    placed = (P(None, "lev", "blk"), P("blk"), P("blk"), P(None, "blk"), P())
    return jax.shard_map(
        local, mesh=mesh, in_specs=placed, out_specs=P(("blk", "lev"), None, None), check_vma=False
    )
```

```python
import functools

import jax
import jax.numpy as jnp
from jax import lax
from jax.experimental import pallas as pl
from jax.experimental.pallas import tpu as pltpu
from jax.sharding import PartitionSpec as P

HALO = 32
CAP = 16
HALF = CAP // 2
LANES = 128
SIDE = LANES // 2
MESH = pl.DeviceIdType.MESH
F32 = jnp.float32
BF16 = jnp.bfloat16
I32 = jnp.int32


def dot_nn(left, right):
    return lax.dot_general(left, right, (((1,), (0,)), ((), ())), preferred_element_type=F32)


def dot_nt(left, right):
    return lax.dot_general(left, right, (((1,), (1,)), ((), ())), preferred_element_type=F32)


def onehot(mask):
    return jnp.where(mask, 1.0, 0.0).astype(BF16)


def rows_of(shape):
    return lax.broadcasted_iota(I32, shape, 0)


def lanes_of(shape):
    return lax.broadcasted_iota(I32, shape, 1)


def both_sides(stack):
    turned = pltpu.roll(stack, SIDE, 1)
    first = lanes_of(stack.shape) < SIDE
    return jnp.where(first, stack, turned).astype(BF16), jnp.where(first, turned, stack).astype(BF16)


def ring(offset, count):
    return min(offset, count - offset)


def kernel(
    blocks, levs,
    io_hbm, io_map_hbm, phys_map_hbm, near_hbm, op_hbm,
    out_ref,
    io_v, io_map_v, phys_map_v, near_v, op_v, weight,
    pick_lo, pick_hi, step_lo, step_hi, step_halo, place_lo, place_hi, cells, halo, partial,
    out_a, mid_a, in_a, out_c, in_c, out_d, in_d,
    load_sem, op_sem, sems, row_sems, halo_sems, lev_sems, row_hello, column_hello, lev_hello,
):
    fields, lev_dev, width = io_v.shape
    rows = blocks * HALF
    total = blocks * width
    shift = width.bit_length() - 1
    me = lax.axis_index("blk")
    my_lev = lax.axis_index("lev")
    side_z = 1 << ((blocks.bit_length() - 1) // 2)
    side_y = blocks // side_z
    shift_z = side_z.bit_length() - 1
    my_y = me >> shift_z
    my_z = me & (side_z - 1)
    chips = levs // 2
    quarter = side_y // 4
    half_tiles = blocks // 2
    half = half_tiles * HALF
    offsets = sorted(
        ((y, z) for y in range(side_y) for z in range(side_z) if y or z),
        key=lambda at: (-ring(at[0], side_y) - ring(at[1], side_z), at),
    )
    lev_offsets = sorted(
        ((x, core) for x in range(chips) for core in range(2) if x or core),
        key=lambda at: (-ring(at[0], chips), at),
    )
    own_tile = quarter * side_z

    def tile_of(y, z):
        return ((y + quarter) % side_y) * side_z + z

    def at_blk(y, z):
        there = (((my_y + y) & (side_y - 1)) << shift_z) | ((my_z + z) & (side_z - 1))
        return there, my_lev

    def at_lev(x, core):
        return (((my_lev >> 1) + x) & (chips - 1)) * 2 + ((my_lev & 1) ^ core)

    def turn(at, count):
        return jnp.where(at < count // 2, at, count // 2 + count - 1 - at)

    row_turn = turn(my_y, side_y)
    lev_turn = turn(my_lev >> 1, chips) * 2 + (my_lev & 1)

    def turn_at_row(y):
        return turn((my_y + y) & (side_y - 1), side_y)

    def turn_at_lev(x, core):
        there = at_lev(x, core)
        return turn(there >> 1, chips) * 2 + (there & 1)

    far_rows = sorted(range(1, side_y), key=lambda at: -ring(at, side_y))
    far_columns = sorted(range(1, side_z), key=lambda at: -ring(at, side_z))

    loads = [
        pltpu.make_async_copy(src, dst, load_sem.at[at])
        for at, (src, dst) in enumerate(
            ((io_map_hbm, io_map_v), (phys_map_hbm, phys_map_v), (io_hbm, io_v), (near_hbm, near_v))
        )
    ]
    for load in loads:
        load.start()

    barrier = pltpu.get_barrier_semaphore()

    def greet(to, semaphore=barrier):
        pl.semaphore_signal(semaphore, inc=1, device_id=to, device_id_type=MESH)

    for y in far_rows:
        pl.when(turn_at_row(y) > row_turn)(functools.partial(greet, at_blk(y, 0)))
    for x, core in lev_offsets:
        pl.when(turn_at_lev(x, core) > lev_turn)(
            functools.partial(greet, (me, at_lev(x, core)))
        )
    for z in range(1, side_z):

        @pl.when(my_z + z < side_z)
        def _():
            for y in far_rows + [0]:
                greet(at_blk(y, z))

    def hear(semaphore, count):
        pl.when(count > 0)(functools.partial(pl.semaphore_wait, semaphore, count))

    hear(barrier, my_z * side_y + row_turn + lev_turn)
    for z in far_columns:
        pl.when(my_z >= z)(functools.partial(greet, at_blk(0, -z), column_hello.at[z - 1]))
    for y in far_rows:
        pl.when(turn_at_row(y) < row_turn)(functools.partial(greet, at_blk(y, 0), row_hello))

    before = onehot(rows_of((width, width)) < lanes_of((width, width)))
    loads[0].wait()
    loads[1].wait()
    codes = []
    members = []
    for ref in (io_map_v, phys_map_v):
        owner = ref[...] >> shift
        to_y = ((owner >> shift_z) - my_y + quarter) & (side_y - 1)
        to_z = ((owner & (side_z - 1)) - my_z) & (side_z - 1)
        tile = (to_y << shift_z) | to_z
        members.append((tile, rows_of((blocks, width)) == tile))
    ranked = dot_nn(
        jnp.concatenate([onehot(members[0][1]), onehot(members[1][1])], axis=0), before
    )
    for at, (tile, member) in enumerate(members):
        part = ranked[at * blocks : (at + 1) * blocks]
        rank = jnp.sum(jnp.where(member, part, 0.0), axis=0, keepdims=True).astype(I32)
        code = tile * HALF + rank
        codes.append(
            (jnp.where(rank < HALF, code, -1), jnp.where(rank >= HALF, code - HALF, -1))
        )

    loads[2].wait()
    meta_row = rows_of((8, width))

    def meta(ref, first):
        slot = (ref[...] & (width - 1)) + 1
        high = (slot >> 5).astype(F32)
        low = (slot & 31).astype(F32)
        return jnp.where(meta_row == first, high, jnp.where(meta_row == first + 1, low, 0.0))

    data = io_v[...].astype(F32).reshape(fields * lev_dev, width)
    one = jnp.concatenate([data, meta(io_map_v, 0)], axis=0)
    own = jnp.concatenate([one, one], axis=0).astype(BF16)
    one = jnp.concatenate([jnp.zeros_like(data), meta(phys_map_v, 2)], axis=0)
    later = jnp.concatenate([one, one], axis=0).astype(BF16)

    def slot_of(y):
        return (y + quarter) % side_y

    def tile_copy(y, z):
        return pltpu.make_async_remote_copy(
            src_ref=out_a.at[slot_of(y), z],
            dst_ref=in_a.at[slot_of(y), z],
            send_sem=sems.at[0 if z else 7],
            recv_sem=sems.at[1 if z else 8],
            device_id=at_blk(y, z),
            device_id_type=MESH,
        )

    first_side = lanes_of((rows, LANES)) < SIDE
    for far in (1, 0):
        where_row = rows_of((half, width)) + far * half
        here = pl.ds(far * half, half)
        pick_lo[here, :] = onehot(where_row == codes[1][0])
        pick_hi[here, :] = onehot(where_row == codes[1][1])
        lo = dot_nt(onehot(where_row == codes[0][0]), own) + dot_nt(pick_lo[here, :], later)
        hi = dot_nt(onehot(where_row == codes[0][1]), own) + dot_nt(pick_hi[here, :], later)
        out_a[pl.ds(far * (side_y // 2), side_y // 2)] = (
            jnp.where(first_side[:half], lo, hi)
            .reshape(side_y // 2, side_z, HALF, LANES).astype(BF16)
        )
        for z in far_columns:

            @pl.when(my_z + z >= side_z)
            def _():
                for y in far_rows + [0]:
                    if slot_of(y) // (side_y // 2) == far:
                        tile_copy(y, z).start()

    for y in far_rows:
        pl.when(turn_at_row(y) < row_turn)(tile_copy(y, 0).start)
    hear(row_hello, side_y - 1 - row_turn)
    for y in far_rows:
        pl.when(turn_at_row(y) > row_turn)(tile_copy(y, 0).start)

    def row_copy(first, count, z, to):
        return pltpu.make_async_remote_copy(
            src_ref=out_a.at[pl.ds(first, count), z],
            dst_ref=mid_a.at[pl.ds(first, count), z],
            send_sem=row_sems.at[z - 1, 0],
            recv_sem=row_sems.at[z - 1, 1],
            device_id=to,
            device_id_type=MESH,
        )

    for z in range(1, side_z):

        @pl.when(my_z + z < side_z)
        def _():
            for y in far_rows:
                row_copy(slot_of(y), 1, z, at_blk(y, 0)).start()

    mid_a[quarter] = out_a[quarter]
    in_a[quarter, 0] = out_a[quarter, 0]

    for x, core in lev_offsets:
        pl.when(turn_at_lev(x, core) < lev_turn)(
            functools.partial(greet, (me, at_lev(x, core)), lev_hello)
        )

    def load_op(l, carry):
        pltpu.make_async_copy(op_hbm.at[:, l], op_v.at[l, pl.ds(0, fields)], op_sem).start()
        return carry

    lax.fori_loop(0, levs, load_op, 0)

    def blk_copy(src, dst, at, far, first, count, to):
        return pltpu.make_async_remote_copy(
            src_ref=src.at[pl.ds(first, count)],
            dst_ref=dst.at[pl.ds(first, count)],
            send_sem=sems.at[at],
            recv_sem=sems.at[at + 1 + far],
            device_id=to,
            device_id_type=MESH,
        )

    def blk_send(src, dst, at, far):
        for y, z in offsets:
            tile = tile_of(y, z)
            if tile // half_tiles == far:
                blk_copy(src, dst, at, far, tile, 1, at_blk(y, z)).start()

    def blk_arrived(src, dst, at, far):
        count = half_tiles - 1 + far
        blk_copy(src, dst, at, far, far * half_tiles, count, at_blk(0, 1)).wait_recv()

    def blk_sent(src, dst, at):
        blk_copy(src, dst, at, 0, 0, blocks - 1, at_blk(0, 1)).wait_send()

    def column_copy(first, count, z):
        return pltpu.make_async_remote_copy(
            src_ref=mid_a.at[:, pl.ds(first, count)],
            dst_ref=in_a.at[:, pl.ds(first, count)],
            send_sem=sems.at[0],
            recv_sem=sems.at[1],
            device_id=at_blk(0, z),
            device_id_type=MESH,
        )

    for z in range(1, side_z):

        @pl.when(my_z + z < side_z)
        def _():
            row_copy(0, side_y - 1, z, at_blk(1, 0)).wait_recv()
            pl.semaphore_wait(column_hello.at[z - 1], 1)
            column_copy(z, 1, z).start()

    loads[3].wait()
    near = (near_v[...] - me * width + HALO) & (total - 1)
    near = jnp.where(
        near < HALO,
        near + width,
        jnp.where((near >= width) & (near < width + HALO), near - width, near),
    )
    wide = (width + 2 * HALO, width)
    spot = rows_of(wide)
    taps = jnp.where(spot == ((lanes_of(wide) + HALO) & (width - 1)), 1.0, 0.0)
    for index in range(4):
        taps = taps + jnp.where(spot == near[index : index + 1], 1.0, 0.0)
    taps = taps.astype(BF16)
    step = dot_nt(pick_lo[...], taps)
    step_lo[...] = step[:, :width].astype(BF16)
    halo_lo = step[:, width:]
    step = dot_nt(pick_hi[...], taps)
    step_hi[...] = step[:, :width].astype(BF16)
    step_halo[...] = jnp.concatenate([halo_lo, step[:, width:]], axis=1).astype(BF16)

    pltpu.make_async_copy(
        op_v.at[:, pl.ds(0, fields)], op_v.at[:, pl.ds(0, fields)], op_sem
    ).wait()
    depth = SIDE

    def spread(l, carry):
        block = op_v[l].astype(F32)
        block = jnp.where(
            lax.broadcasted_iota(I32, block.shape, 0) < fields, block, 0.0
        ).reshape(depth, block.shape[2])
        weight[pl.ds(pl.multiple_of(l * depth, depth), depth), :] = block.astype(BF16)
        return carry

    lax.fori_loop(0, levs, spread, 0)

    choose_row = rows_of((8, LANES))
    choose_lane = lanes_of((8, LANES))
    choose = jnp.zeros((8, LANES), F32)
    for at, lane in enumerate((56, 56 + SIDE, 58, 58 + SIDE)):
        here = choose_row == at
        choose = jnp.where(here & (choose_lane == lane), 32.0, choose)
        choose = jnp.where(here & (choose_lane == lane + 1), 1.0, choose)
    choose = choose.astype(BF16)

    row_tiles = pltpu.make_async_remote_copy(
        src_ref=out_a.at[pl.ds(0, side_y - 1), 0],
        dst_ref=in_a.at[pl.ds(0, side_y - 1), 0],
        send_sem=sems.at[7],
        recv_sem=sems.at[8],
        device_id=at_blk(1, 0),
        device_id_type=MESH,
    )

    edge = 2 * HALO
    row_tiles.wait_recv()
    column_copy(1, side_z - 1, 1).wait_recv()
    stack = in_a[...].astype(F32).reshape(rows, LANES)
    sides = both_sides(stack)
    slots = dot_nt(choose, stack.astype(BF16)).astype(I32)

    def found(first, count):
        target = ((rows_of((count, rows)) + (first + width - HALO)) & (width - 1)) + 1
        return (
            dot_nn(onehot(target == slots[0:1]), sides[0])
            + dot_nn(onehot(target == slots[1:2]), sides[1])
        ).astype(BF16)

    cells[pl.ds(0, edge), :] = found(0, edge)

    up = pltpu.make_async_remote_copy(
        src_ref=cells.at[pl.ds(0, HALO)],
        dst_ref=halo.at[pl.ds(0, HALO)],
        send_sem=halo_sems.at[0],
        recv_sem=halo_sems.at[1],
        device_id=((me + 1) & (blocks - 1), my_lev),
        device_id_type=MESH,
    )
    down = pltpu.make_async_remote_copy(
        src_ref=cells.at[pl.ds(HALO, HALO)],
        dst_ref=halo.at[pl.ds(HALO, HALO)],
        send_sem=halo_sems.at[2],
        recv_sem=halo_sems.at[3],
        device_id=((me + blocks - 1) & (blocks - 1), my_lev),
        device_id_type=MESH,
    )
    up.start()
    down.start()

    if width > edge:
        rest = width - edge
        cells[pl.ds(edge, rest), :] = found(edge, rest)
    lo = dot_nn(step_lo[...], cells[...])
    hi = dot_nn(step_hi[...], cells[...])
    partial[...] = jnp.where(first_side, lo, hi)

    up.wait_recv()
    down.wait_recv()
    beside = halo[...]
    on_side = lanes_of(beside.shape) < SIDE
    none = jnp.zeros_like(beside)
    beside = jnp.concatenate(
        [jnp.where(on_side, beside, none), jnp.where(on_side, none, beside)], axis=0
    )
    for far in (1, 0):
        here = pl.ds(far * half, half)
        summed = partial[here, :] + dot_nn(step_halo[here, :], beside)
        out_c[pl.ds(far * half_tiles, half_tiles)] = (
            (0.2 * summed).reshape(half_tiles, HALF, LANES).astype(BF16)
        )
        blk_send(out_c, in_c, 3, far)
    in_c[own_tile] = out_c[own_tile]

    per = levs * CAP
    line = rows_of((per, rows))
    line = (line >> 4) * (2 * CAP) + (line & (CAP - 1)) + 1
    place_lo[0:per, :] = onehot(line == slots[2:3])
    place_hi[0:per, :] = onehot(line == slots[3:4])
    place_lo[per : 2 * per, :] = onehot(line + CAP == slots[2:3])
    place_hi[per : 2 * per, :] = onehot(line + CAP == slots[3:4])

    def opened(buffer, far):
        stack = buffer[pl.ds(far * half_tiles, half_tiles)].astype(F32).reshape(half, LANES)
        return both_sides(stack)

    blk_arrived(out_c, in_c, 3, 0)
    sides = opened(in_c, 0)
    partial[...] = dot_nn(place_lo[:, :half], sides[0]) + dot_nn(place_hi[:, :half], sides[1])
    blk_arrived(out_c, in_c, 3, 1)
    sides = opened(in_c, 1)
    placed = partial[...] + (
        dot_nn(place_lo[:, half:], sides[0]) + dot_nn(place_hi[:, half:], sides[1])
    )
    out_d[...] = (
        jnp.where(lanes_of((per, LANES)) < SIDE, placed[:per], placed[per:])
        .reshape(levs, CAP, LANES).astype(BF16)
    )

    hear(lev_hello, levs - 1 - lev_turn)
    for x, core in lev_offsets:
        to = at_lev(x, core)
        pltpu.make_async_remote_copy(
            src_ref=out_d.at[to],
            dst_ref=in_d.at[my_lev],
            send_sem=sems.at[6],
            recv_sem=lev_sems.at[x],
            device_id=(me, to),
            device_id_type=MESH,
        ).start()
    in_d[my_lev] = out_d[my_lev]

    def lev_wait(x, count):
        return pltpu.make_async_remote_copy(
            src_ref=out_d.at[pl.ds(0, count)],
            dst_ref=in_d.at[pl.ds(0, count)],
            send_sem=sems.at[6],
            recv_sem=lev_sems.at[x],
            device_id=(me, at_lev(0, 1)),
            device_id_type=MESH,
        )

    side = lanes_of((CAP, LANES)) < SIDE
    result = None
    for x in sorted(range(chips), key=lambda at: ring(at, chips)):
        lev_wait(x, 2 if x else 1).wait_recv()
        chip = ((my_lev >> 1) - x) & (chips - 1)
        even = in_d[2 * chip].astype(F32)
        odd = in_d[2 * chip + 1].astype(F32)
        upper = jnp.where(side, even, pltpu.roll(odd, SIDE, 1))
        lower = jnp.where(side, pltpu.roll(even, SIDE, 1), odd)
        columns = jnp.concatenate([upper, lower], axis=0).astype(BF16)
        term = dot_nn(columns, weight[pl.ds(pl.multiple_of(chip * LANES, LANES), LANES), :])
        result = term if result is None else result + term
    size = levs * lev_dev
    for field in range(fields):
        out_ref[field] = result[:, field * size : (field + 1) * size]

    row_tiles.wait_send()
    column_copy(1, side_z - 1, 1).wait_send()
    for z in range(1, side_z):
        pl.when(my_z + z < side_z)(row_copy(0, side_y - 1, z, at_blk(1, 0)).wait_send)
    up.wait_send()
    down.wait_send()
    blk_sent(out_c, in_c, 3)
    lev_wait(0, levs - 1).wait_send()


def local(io_data, io_map, phys_map, neighbours, column_op):
    fields, lev_dev, width = io_data.shape
    blocks = lax.axis_size("blk")
    levs = lax.axis_size("lev")
    rows = blocks * HALF
    count = width // levs
    span = fields * levs * lev_dev
    side_z = 1 << ((blocks.bit_length() - 1) // 2)
    side_y = blocks // side_z
    any_space = pl.BlockSpec(memory_space=pl.ANY)
    result = pl.pallas_call(
        functools.partial(kernel, blocks, levs),
        out_shape=jax.ShapeDtypeStruct((fields, count, levs * lev_dev), F32),
        in_specs=[any_space] * 5,
        out_specs=pl.BlockSpec(memory_space=pltpu.VMEM),
        scratch_shapes=[
            pltpu.VMEM((fields, lev_dev, width), BF16),
            pltpu.VMEM((1, width), I32),
            pltpu.VMEM((1, width), I32),
            pltpu.VMEM((4, width), I32),
            pltpu.VMEM((levs, fields + 1, lev_dev, span), BF16),
            pltpu.VMEM((levs * SIDE, span), BF16),
            pltpu.VMEM((rows, width), BF16),
            pltpu.VMEM((rows, width), BF16),
            pltpu.VMEM((rows, width), BF16),
            pltpu.VMEM((rows, width), BF16),
            pltpu.VMEM((rows, 4 * HALO), BF16),
            pltpu.VMEM((width, rows), BF16),
            pltpu.VMEM((width, rows), BF16),
            pltpu.VMEM((width, LANES), BF16),
            pltpu.VMEM((2 * HALO, LANES), BF16),
            pltpu.VMEM((width, LANES), F32),
            pltpu.VMEM((side_y, side_z, HALF, LANES), BF16),
            pltpu.VMEM((side_y, side_z, HALF, LANES), BF16),
            pltpu.VMEM((side_y, side_z, HALF, LANES), BF16),
            pltpu.VMEM((blocks, HALF, LANES), BF16),
            pltpu.VMEM((blocks, HALF, LANES), BF16),
            pltpu.VMEM((levs, CAP, LANES), BF16),
            pltpu.VMEM((levs, CAP, LANES), BF16),
            pltpu.SemaphoreType.DMA((4,)),
            pltpu.SemaphoreType.DMA,
            pltpu.SemaphoreType.DMA((9,)),
            pltpu.SemaphoreType.DMA((side_z - 1, 2)),
            pltpu.SemaphoreType.DMA((4,)),
            pltpu.SemaphoreType.DMA((levs // 2,)),
            pltpu.SemaphoreType.REGULAR,
            pltpu.SemaphoreType.REGULAR((side_z - 1,)),
            pltpu.SemaphoreType.REGULAR,
        ],
        compiler_params=pltpu.CompilerParams(
            collective_id=0, has_side_effects=True, vmem_limit_bytes=60 * 1024 * 1024
        ),
    )(
        io_data,
        io_map.reshape(1, width),
        phys_map.reshape(1, width),
        neighbours,
        column_op.reshape(fields, levs, lev_dev, span),
    )
    return jnp.transpose(result, (1, 0, 2))


def solution(mesh):
    placed = (P(None, "lev", "blk"), P("blk"), P("blk"), P(None, "blk"), P())
    return jax.shard_map(
        local, mesh=mesh, in_specs=placed, out_specs=P(("blk", "lev"), None, None), check_vma=False
    )
```
